512 devices in a mesh: sect: 4 (over y), seq: 128 (over z, x, core).
Axes of the slice: x: 4, y: 4, z: 16, core: 2. Of those that a mesh axis runs over, the one named last changes fastest.
Arguments:
- tokens: bfloat16 [1024, 6144], P('seq'), may hold values from -6 to 6
- routes: int32 [1024, 2], P('seq'), may hold values from 0 to 7, all different within a row; in each aligned block of 8 rows (0 to 7, 8 to 15, ...) at most 3 rows name the same one
- w_router: bfloat16 [6144, 8], replicated, may hold values from -0.078125 to 0.078125
- w_gate: bfloat16 [6144, 65536], P(None, ('seq', 'sect')), may hold values from -0.078125 to 0.078125
- w_up: bfloat16 [6144, 65536], P(None, ('seq', 'sect')), may hold values from -0.078125 to 0.078125
- cotangent: bfloat16 [384, 65536], P(None, ('seq', 'sect')), may hold values from -6 to 6
Outputs:
- hidden: bfloat16 [384, 65536], P(None, ('seq', 'sect'))
- grad_tokens: bfloat16 [1024, 6144], P('seq')
- grad_router: float32 [6144, 8], replicated
The draws below stay inside these ranges and needn't reach their ends.
Inputs may be any that keep to these rules, and one draw needn't show every extreme that they name: `routes`: the two experts of a token differ. Among the tokens of one index of seq (aligned blocks of 8 tokens) no expert is named more than 3 times, and in every draw some block names some expert exactly 3 times.
All inputs are finite; a program needn't handle non-finite values.
Results may differ from the reference program's by a relative error of at most 0.0055.
Values may be sent and summed in bfloat16 or wider, within the bound.
No kernel may reach another device: no remote copies, remote signals or barrier semaphores. Data moves between devices by JAX's collectives and lax.ppermute only.
A program may use at most 128 MiB of HBM per device.

```python
import math
import jax
import jax.numpy as jnp
import numpy as np
from jax import lax

D = 6144
EXPERTS = 8
FFW = 8192
TOK_DEV = 8
MOST = 3
SLOTS = 384
TOKENS = 1024
N_SEQ = 128


def steps_of(rng, shape, shards, smallest, largest):
    def one(position, shards_of):
        draws = jax.random.uniform(jax.random.fold_in(jax.random.fold_in(rng, 6), position), (shards_of,), jnp.float32, smallest / len(shards), largest / len(shards))
        return jnp.repeat(jnp.exp(draws), shape[position] // shards_of).reshape((-1,) + (1,) * (len(shape) - position - 1))

    factor_of = one(*shards[0])
    for cut in shards[1:]:
        factor_of = factor_of * one(*cut)
    return factor_of


def routed_block(stream_key, own, number, rows, number_of, top, limit, lean):
    order = jax.random.permutation(stream_key, number_of)
    crowded, usual = portions_of(number_of, rows * top, limit, lean, True), portions_of(number_of, rows * top, limit, lean, False)
    places = jnp.arange(number_of)

    def named(lengths, offset_by):
        used = int((lengths > 0).sum())
        fixed = max(1, used // 4)
        moved = fixed + (places - fixed + offset_by * (used - fixed)) % max(1, number_of - fixed)
        return jnp.zeros((number_of,), jnp.int32).at[order[jnp.where(places < fixed, places, moved)]].set(jnp.asarray(lengths, jnp.int32))

    lengths = jnp.where(number % 4 == 0, named(crowded, number // 4), named(usual, number - number // 4 - 1))
    mixed = jax.random.permutation(jax.random.fold_in(own, 3), number_of)
    giver, receiver = mixed[0:number_of // 2 * 2:2], mixed[1:number_of // 2 * 2:2]
    margin = jnp.minimum(lengths[giver] - 1, limit - lengths[receiver]) // 2
    margin = jnp.where((giver == order[0]) | (receiver == order[0]) | (lengths[receiver] == 0), 0, jnp.maximum(margin, 0))
    moved = jax.random.randint(jax.random.fold_in(own, 4), (number_of // 2,), 0, 1 << 20) % (margin + 1)
    lengths = lengths.at[giver].add(-moved).at[receiver].add(moved)
    members = jnp.searchsorted(jnp.cumsum(lengths), jnp.arange(rows * top), side="right").astype(jnp.int32)
    table = members.reshape(top, rows).T
    table = table[jax.random.permutation(jax.random.fold_in(own, 1), rows)]
    offset_by = jax.random.randint(jax.random.fold_in(own, 2), (rows, 1), 0, top)
    return jnp.take_along_axis(table, (jnp.arange(top)[None, :] + offset_by) % top, axis=1)


def portions_of(count, total, limit, skew, full):
    weights = [(1 << 20) // math.isqrt(grade ** skew) + 1 for grade in range(1, count + 1)]
    largest = limit if full else min(limit, max(-(-total // count), total * weights[0] // sum(weights)))
    least = 1 if total - largest >= count - 1 else 0
    given, surplus = [largest] + [least] * (count - 1), total - largest - least * (count - 1)
    while surplus > 0:
        movable = [i for i in range(1, count) if given[i] < largest] or [i for i in range(1, count) if given[i] < limit]
        pool, remaining = sum([weights[i] for i in movable]), surplus
        for i in movable:
            addition = min(limit - given[i], max(1, remaining * weights[i] // pool), surplus)
            given[i] = given[i] + addition
            surplus = surplus - addition
    return np.array(given)


def normal_values(own_key, shape, deviation, limit, cuts=(), kind=jnp.bfloat16):
    array = deviation * jax.random.normal(own_key, shape, jnp.float32)
    if cuts:
        array = array * steps_of(own_key, shape, cuts, -0.22, 0.18)
    return jnp.clip(array, -limit, limit).astype(kind)


def setup_inputs(seed: int = 0) -> dict:
    arg_keys = jax.random.split(jax.random.key(seed), 7)
    tokens = normal_values(arg_keys[0], (TOKENS, D), 1.0, 6.0, ((0, 128),))
    routes_keys = jax.random.split(jax.random.fold_in(arg_keys[1], 1), TOKENS // TOK_DEV)
    routes_turns = jax.random.permutation(jax.random.fold_in(arg_keys[1], 3), TOKENS // TOK_DEV)
    routes = jax.vmap(lambda own, number: routed_block(jax.random.fold_in(arg_keys[1], 2), own, number, TOK_DEV, EXPERTS, 2, MOST, 2))(routes_keys, routes_turns).reshape((TOKENS, 2))
    w_router = normal_values(arg_keys[2], (D, EXPERTS), D ** -0.5, 0.078125)
    w_gate = normal_values(arg_keys[3], (D, EXPERTS * FFW), D ** -0.5, 0.078125, ((1, 512),))
    w_up = normal_values(arg_keys[4], (D, EXPERTS * FFW), D ** -0.5, 0.078125, ((1, 512),))
    cotangent = normal_values(arg_keys[5], (SLOTS, EXPERTS * FFW), 1.0, 6.0, ((1, 512),))
    return dict(tokens=tokens, routes=routes, w_router=w_router, w_gate=w_gate, w_up=w_up, cotangent=cotangent)


highest = lax.Precision.HIGHEST


def reference(tokens, routes, w_router, w_gate, w_up, cotangent):
    pairs = routes.reshape(N_SEQ, TOK_DEV * 2)
    onehot = (pairs[:, :, None] == jnp.arange(EXPERTS, dtype=jnp.int32)[None, None, :]).astype(jnp.int32)
    ranks = jnp.sum((jnp.cumsum(onehot, axis=1) - 1) * onehot, axis=2)
    places = (jnp.arange(N_SEQ, dtype=jnp.int32)[:, None] * MOST + ranks).reshape(-1)
    expert_ids = pairs.reshape(-1)
    select = ((expert_ids[None, None, :] == jnp.arange(EXPERTS, dtype=jnp.int32)[:, None, None])
              & (places[None, None, :] == jnp.arange(SLOTS, dtype=jnp.int32)[None, :, None])).astype(jnp.float32)
    logits = jnp.dot(tokens, w_router, preferred_element_type=jnp.float32)
    choose = (routes[:, :, None] == jnp.arange(EXPERTS, dtype=jnp.int32)[None, None, :]).astype(jnp.float32)
    picked = jnp.sum(choose * logits[:, None, :], axis=2)
    probs = jax.nn.softmax(picked, axis=1)
    pair_rows = jnp.repeat(tokens, 2, axis=0).astype(jnp.float32)
    flat_probs = probs.reshape(-1)

    def one_expert(index):
        chooser = select[index]
        rows = jnp.dot(chooser, pair_rows, precision=highest).astype(jnp.bfloat16)
        weight_low = jnp.dot(chooser, flat_probs, precision=highest).astype(jnp.bfloat16)
        slot_weight = lax.optimization_barrier(weight_low).astype(jnp.float32)[:, None]
        gate_cols = lax.dynamic_slice_in_dim(w_gate, index * FFW, FFW, 1)
        up_cols = lax.dynamic_slice_in_dim(w_up, index * FFW, FFW, 1)
        gate_pre = jnp.dot(rows, gate_cols, preferred_element_type=jnp.float32)
        up_pre = jnp.dot(rows, up_cols, preferred_element_type=jnp.float32)
        sigma = jax.nn.sigmoid(gate_pre)
        act = gate_pre * sigma * up_pre
        hidden_part = (slot_weight * act).astype(jnp.bfloat16)
        grad_out = lax.dynamic_slice_in_dim(cotangent, index * FFW, FFW, 1).astype(jnp.float32)
        slot_dp = jnp.sum(grad_out * act, axis=1)
        d_gate = (grad_out * slot_weight * up_pre * sigma * (1.0 + gate_pre * (1.0 - sigma))).astype(jnp.bfloat16)
        d_up = (grad_out * slot_weight * gate_pre * sigma).astype(jnp.bfloat16)
        dims = (((1,), (1,)), ((), ()))
        slot_dx = lax.dot_general(d_gate, gate_cols, dims, preferred_element_type=jnp.float32)
        slot_dx = slot_dx + lax.dot_general(d_up, up_cols, dims, preferred_element_type=jnp.float32)
        return hidden_part, slot_dx, slot_dp

    hidden_all, slot_dx, slot_dp = lax.map(one_expert, jnp.arange(EXPERTS, dtype=jnp.int32))
    hidden = jnp.transpose(hidden_all, (1, 0, 2)).reshape(SLOTS, EXPERTS * FFW)
    pair_dx = jnp.einsum('esq,esd->qd', select, slot_dx, precision=highest)
    token_dx = pair_dx.reshape(TOKENS, 2, D).sum(axis=1)
    pair_dp = jnp.einsum('esq,es->q', select, slot_dp, precision=highest).reshape(TOKENS, 2)
    mean_dp = jnp.sum(probs * pair_dp, axis=1, keepdims=True)
    d_pick = probs * (pair_dp - mean_dp)
    d_logits = jnp.sum(choose * d_pick[:, :, None], axis=1)
    router_dx = jnp.dot(d_logits, w_router.astype(jnp.float32).T, precision=highest)
    grad_tokens = (token_dx + router_dx).astype(jnp.bfloat16)
    grad_router = jnp.dot(tokens.astype(jnp.float32).T, d_logits, precision=highest)
    return hidden, grad_tokens, grad_router
```

```python
import jax
import jax.numpy as jnp
from jax import lax
from jax.experimental import pallas as pl
from jax.experimental.pallas import tpu as pltpu
from jax.sharding import Mesh, PartitionSpec as P

AXES = ("sect", "e", "zl", "x", "core")
bf16, f32, i32 = jnp.bfloat16, jnp.float32, jnp.int32
Y, E, Z, X, C = 4, 8, 2, 4, 2
MOST = 3
LIMIT = 48 * 1024 * 1024


def iota(shape, dim):
    return lax.broadcasted_iota(i32, shape, dim)


def split2(v):
    hi = v.astype(bf16).astype(f32)
    return hi, v - hi


def pre_kernel(rows_ref, w_ref, own_ref, part_ref):
    step = pl.program_id(0)
    rows = jnp.concatenate([rows_ref[i, 0:96, :] for i in range(X)], axis=0)
    got = jnp.dot(rows, w_ref[...], preferred_element_type=f32)
    own = jnp.concatenate([got[:, 0:256], got[:, 512:640]], axis=1)
    part = got[:, 256:640]

    @pl.when(step == 0)
    def _():
        own_ref[...] = own
        part_ref[...] = part

    @pl.when(step != 0)
    def _():
        own_ref[...] += own
        part_ref[...] += part


def act_kernel(expert_ref, own_ref, recv_ref, cot_ref, rows_ref, hidden_ref, d_ref, coef_ref):
    slots = own_ref.shape[0]
    gate = own_ref[:, 0:128] + recv_ref[:, 0:128]
    up = own_ref[:, 128:256] + recv_ref[:, 128:256]
    logits = own_ref[:, 256:384] + recv_ref[:, 256:384]
    eye = iota((96, 128), 0) == iota((96, 128), 1)
    other = jnp.concatenate(
        [
            jnp.sum(
                jnp.where(eye, rows_ref[i, 96:104, 0:128].astype(f32)[0:1, :], 0.0),
                axis=1,
                keepdims=True,
            )
            for i in range(X)
        ],
        axis=0,
    )
    lane = iota((slots, 128), 1)
    valid = other > 0.5
    mine = lane == expert_ref[0]
    its = lane == (other - 1.0).astype(i32)
    own_logit = jnp.sum(jnp.where(mine, logits, 0.0), axis=1, keepdims=True)
    other_logit = jnp.sum(jnp.where(its, logits, 0.0), axis=1, keepdims=True)
    top = jnp.maximum(own_logit, other_logit)
    a, b = jnp.exp(own_logit - top), jnp.exp(other_logit - top)
    prob = jnp.where(valid, a / (a + b), 0.0)
    both = jnp.where(valid, (a / (a + b)) * (b / (a + b)), 0.0)
    weight = prob.astype(bf16).astype(f32)
    sigma = jax.nn.sigmoid(gate)
    act = gate * sigma * up
    hidden_ref[...] = (weight * act).astype(bf16)
    grad_out = cot_ref[...].astype(f32)
    dp = jnp.sum(grad_out * act, axis=1, keepdims=True)
    d_gate = grad_out * weight * up * sigma * (1.0 + gate * (1.0 - sigma))
    d_up = grad_out * weight * gate * sigma
    hi, rest = split2(dp)
    lo, last = split2(rest)
    d_ref[:, 0:128] = d_gate.astype(bf16)
    d_ref[:, 128:256] = d_up.astype(bf16)
    d_ref[:, 256:384] = jnp.where(
        lane == 0, hi, jnp.where(lane == 1, lo, jnp.where(lane == 2, last, 0.0))
    ).astype(bf16)
    third = lane % E
    used = lane < 3 * E
    sign = jnp.where(third == expert_ref[0], 1.0, 0.0) - jnp.where(
        third == (other - 1.0).astype(i32), 1.0, 0.0
    )
    coef_ref[...] = jnp.where(used, sign * both, 0.0)


def dx_kernel(d_ref, recv_ref, coef_ref, w_ref, rows_ref, out_ref):
    slots = d_ref.shape[0]
    rows = jnp.concatenate([rows_ref[i, 0:96, :] for i in range(X)], axis=0)
    dims = (((1,), (1,)), ((), ()))
    dx = lax.dot_general(d_ref[:, 0:256], w_ref[:, 0:256], dims, preferred_element_type=f32)
    dx = dx + lax.dot_general(
        recv_ref[:, 0:256], w_ref[:, 256:512], dims, preferred_element_type=f32
    )
    dp = jnp.sum(d_ref[:, 256:384].astype(f32), axis=1, keepdims=True)
    dp_recv = jnp.sum(recv_ref[:, 256:384].astype(f32), axis=1, keepdims=True)
    coef = coef_ref[...] * (dp + dp_recv)
    hi, rest = split2(coef)
    lo, last = split2(rest)
    lane = iota((slots, 128), 1)
    three = jnp.where(lane < E, hi, jnp.where(lane < 2 * E, lo, last)).astype(bf16)
    got = lax.dot_general(three, rows, (((0,), (0,)), ((), ())), preferred_element_type=f32)
    router = got[0:E] + got[E : 2 * E] + got[2 * E : 3 * E]
    router_hi, router_lo = split2(router)
    dp_hi, dp_lo = split2(dp)
    eye = iota((96, 128), 0) == iota((96, 128), 1)
    width = dx.shape[1]
    for i in range(X):
        part = slice(i * 96, (i + 1) * 96)
        out_ref[i, 0:96, :] = dx[part].astype(bf16)
        dp_row = [
            jnp.pad(
                jnp.sum(jnp.where(eye, v[part], 0.0), axis=0, keepdims=True),
                ((0, 0), (0, width - 128)),
            )
            for v in (dp_hi, dp_lo)
        ]
        meta = jnp.concatenate(
            [
                router_hi[2 * i : 2 * i + 2],
                router_lo[2 * i : 2 * i + 2],
                *dp_row,
                jnp.zeros((2, width), f32),
            ],
            axis=0,
        )
        out_ref[i, 96:104, :] = meta.astype(bf16)


def sum_kernel(recv_ref, out_ref, acc_ref):
    step = pl.program_id(0)
    total = jnp.sum(recv_ref[...].astype(f32), axis=0)

    @pl.when(step == 0)
    def _():
        acc_ref[...] = total

    @pl.when(step != 0)
    def _():
        acc_ref[...] += total

    @pl.when(step == pl.num_programs(0) - 1)
    def _():
        main = acc_ref[0:96, :]
        meta = acc_ref[96:104, :]
        router_hi, router_lo = split2(meta[0:2] + meta[2:4])
        dp_hi, dp_lo = split2(meta[4:5, 0:128] + meta[5:6, 0:128])
        dp_row = jnp.concatenate([jnp.zeros((1, 512), f32), dp_hi, dp_lo], axis=1)
        source = jnp.concatenate(
            [main, router_hi, router_lo, dp_row, jnp.zeros((3, 768), f32)], axis=0
        ).astype(bf16)
        row = iota((256, 104), 0)
        column = iota((256, 104), 1)
        place, q = row // 8, row % 8
        core = place % 2

        def pick(cases):
            target = jnp.full((256, 104), -1, i32)
            for value, where in cases:
                target = jnp.where(q == value, where, target)
            return jnp.where(column == target, 1.0, 0.0).astype(bf16)

        hi, lo, dp = 96 + core, 98 + core, 100
        first = pick(
            [(0, 3 * place), (1, 3 * place + 1), (2, 3 * place + 2), (5, hi), (6, lo)]
        )
        left = pick([(3, 3 * place), (4, 3 * place + 2), (7, lo)])
        right = pick([(3, 3 * place + 1), (4, hi), (7, jnp.full((256, 104), dp, i32))])
        got = jnp.dot(first, source[:, 0:512], preferred_element_type=f32)
        tail = source[:, 512:768]
        out_ref[:, 0:256] = (
            got[:, 0:256] + jnp.dot(left, tail, preferred_element_type=f32)
        ).astype(bf16)
        out_ref[:, 256:512] = (
            got[:, 256:512] + jnp.dot(right, tail, preferred_element_type=f32)
        ).astype(bf16)


def call(kernel, grid, in_specs, out_specs, out_shape, scratch=()):
    return pl.pallas_call(
        kernel,
        grid=grid,
        in_specs=in_specs,
        out_specs=out_specs,
        out_shape=out_shape,
        scratch_shapes=list(scratch),
        compiler_params=pltpu.CompilerParams(vmem_limit_bytes=LIMIT),
    )


def whole(*shape):
    return pl.BlockSpec(shape, lambda *_: (0,) * len(shape))


def a2a(v, axes):
    return lax.all_to_all(v, axes, split_axis=0, concat_axis=0, tiled=True)


def everywhere(v, count):
    return jnp.broadcast_to(v[None], (count,) + v.shape)


def swap(v):
    return lax.ppermute(v, "core", [(0, 1), (1, 0)])


def local(tokens, routes, w_router, w_gate, w_up, cotangent):
    tok, width = tokens.shape
    half, piece = width // C, width // (C * Y)
    core, sect, expert = lax.axis_index("core"), lax.axis_index("sect"), lax.axis_index("e")
    slots = cotangent.shape[0]
    sds = jax.ShapeDtypeStruct

    pairs = routes.reshape(-1)
    count = tok * 2
    same = pairs[:, None] == pairs[None, :]
    earlier = jnp.arange(count)[None, :] < jnp.arange(count)[:, None]
    ranks = jnp.sum((same & earlier).astype(i32), axis=1)
    places = pairs * MOST + ranks
    select = (places[None, :] == jnp.arange(E * MOST, dtype=i32)[:, None]).astype(f32)
    others = routes[:, ::-1].reshape(-1).astype(f32) + 1.0
    other_of = jnp.sum(select * others[None, :], axis=1)
    by_token = jnp.sum(select.reshape(E * MOST, tok, 2), axis=2).astype(bf16)

    mine = lax.dynamic_index_in_dim(
        tokens.reshape(tok, C, Y, piece), sect, axis=2, keepdims=False
    ).reshape(tok, C * piece)
    picked = jnp.dot(by_token, mine, preferred_element_type=f32).astype(bf16)
    picked = picked.reshape(E, MOST, C, piece).transpose(0, 2, 1, 3)
    note = jnp.pad(other_of.reshape(E, 1, 1, MOST), ((0, 0), (0, 0), (0, 0), (0, piece - MOST)))
    note = jnp.broadcast_to(note, (E, C, 1, piece)).astype(bf16)
    out = jnp.concatenate([picked, note], axis=2)
    out = jnp.broadcast_to(out[:, None], (E, Z, C, MOST + 1, piece))
    arrived = a2a(out.reshape(E * Z * C, MOST + 1, piece), ("e", "zl", "core"))

    block = arrived[:, 0:MOST, :].reshape(E * Z * C * MOST, piece)
    notes = arrived[:, MOST, 0:MOST].reshape(1, E * Z * C * MOST)
    notes = jnp.pad(notes, ((0, 7), (0, piece - E * Z * C * MOST)))
    block = jnp.concatenate([block, notes], axis=0)
    rows = a2a(everywhere(block, Y * X), ("sect", "x"))

    both = jnp.concatenate([w_gate, w_up], axis=1)
    own_w = lax.dynamic_slice_in_dim(both, core * half, half, 0)
    sent_w = lax.dynamic_slice_in_dim(both, (1 - core) * half, half, 0)
    router_half = lax.dynamic_slice_in_dim(w_router, core * half, half, 0)
    weights = jnp.concatenate(
        [own_w, swap(sent_w), jnp.pad(router_half, ((0, 0), (0, 128 - E)))], axis=1
    )
    cot = cotangent.reshape(E * Z, X, C * MOST, 128).transpose(1, 0, 2, 3).reshape(slots, 128)

    rows_spec = pl.BlockSpec((X, 104, piece), lambda i: (i, 0, 0))
    w_spec = pl.BlockSpec((piece, 640), lambda i: (i, 0))
    own, part = call(
        pre_kernel,
        (Y,),
        [rows_spec, w_spec],
        [whole(slots, 384), whole(slots, 384)],
        [sds((slots, 384), f32), sds((slots, 384), f32)],
    )(rows, weights)
    hidden, d, coef = call(
        act_kernel,
        (1,),
        [
            pl.BlockSpec(memory_space=pltpu.SMEM),
            whole(slots, 384),
            whole(slots, 384),
            whole(slots, 128),
            whole(X, 104, piece),
        ],
        [whole(slots, 128), whole(slots, 384), whole(slots, 128)],
        [sds((slots, 128), bf16), sds((slots, 384), bf16), sds((slots, 128), f32)],
    )(expert.reshape(1).astype(i32), own, swap(part), cot, rows)
    hidden = hidden.reshape(X, E * Z, C * MOST, 128).transpose(1, 0, 2, 3).reshape(slots, 128)

    back = call(
        dx_kernel,
        (Y,),
        [whole(slots, 384), whole(slots, 384), whole(slots, 128), w_spec, rows_spec],
        rows_spec,
        sds((Y * X, 104, piece), bf16),
    )(d, swap(d), coef, weights, rows)

    back = a2a(back, ("sect", "x"))
    summed = call(
        sum_kernel,
        (Y,),
        [rows_spec],
        whole(256, 512),
        sds((256, 512), bf16),
        [pltpu.VMEM((104, piece), f32)],
    )(back)
    home = a2a(summed.reshape(E * Z * C, 8, 512), ("e", "zl", "core"))
    home = home.reshape(E, Z, C, 8, 512)

    tails = [home[:, :, :, 3, 0:256], home[:, :, :, 3, 256:512], home[:, :, :, 4, 0:256]]
    main = jnp.concatenate([home[:, :, :, 0:3, :], jnp.stack(tails, axis=3)], axis=4)
    spread = by_token.T.reshape(tok, E, MOST)
    token_dx = jnp.einsum("ter,ezcrd->tcd", spread, main, preferred_element_type=f32)
    router_parts = jnp.concatenate(
        [
            home[:, :, :, 5, :].astype(f32) + home[:, :, :, 6, :].astype(f32),
            home[:, :, :, 4, 256:512].astype(f32) + home[:, :, :, 7, 0:256].astype(f32),
        ],
        axis=3,
    )
    router = jnp.sum(router_parts, axis=(0, 1))
    dp = jnp.sum(home[:, :, :, 7, 256:512].astype(f32), axis=(1, 2))
    dp = dp[:, 0:128] + dp[:, 128:256]
    place = (expert * Z + lax.axis_index("zl")) * C + core
    dp = lax.dynamic_slice_in_dim(dp, place * MOST, MOST, 1).reshape(E * MOST)
    pair_dp = jnp.sum(select * dp[:, None], axis=0).reshape(tok, 2)

    logits = jnp.dot(tokens, w_router, preferred_element_type=f32)
    choose = (routes[:, :, None] == jnp.arange(E, dtype=i32)[None, None, :]).astype(f32)
    probs = jax.nn.softmax(jnp.sum(choose * logits[:, None, :], axis=2), axis=1)
    mean_dp = jnp.sum(probs * pair_dp, axis=1, keepdims=True)
    d_pick = probs * (pair_dp - mean_dp)
    d_logits = jnp.sum(choose * d_pick[:, :, None], axis=1)
    w_mine = lax.dynamic_index_in_dim(
        w_router.reshape(C, Y, piece, E), sect, axis=1, keepdims=False
    ).astype(f32)
    router_dx = jnp.einsum("te,cde->tcd", d_logits, w_mine, precision=lax.Precision.HIGHEST)
    grad_tokens = (token_dx + router_dx).astype(bf16).reshape(tok, C * piece)

    router = router.reshape(1, C * piece)
    hi = lax.reduce_precision(router, 8, 7)
    lo = router - hi
    pack = jnp.concatenate([grad_tokens, hi.astype(bf16), lo.astype(bf16)], axis=0)
    got = a2a(everywhere(pack, Y), ("sect",))
    grad_tokens = got[:, 0:tok, :].reshape(Y, tok, C, piece).transpose(1, 2, 0, 3)
    mine_router = got[:, tok, :].astype(f32) + got[:, tok + 1, :].astype(f32)
    mine_router = mine_router.reshape(Y, C, piece).transpose(1, 0, 2).reshape(8, width // 8)
    grad_router = a2a(everywhere(mine_router, X * C), ("x", "core"))
    return hidden, grad_tokens.reshape(tok, width), grad_router.reshape(E, width).T


def solution(mesh):
    fine = Mesh(mesh.devices.reshape(Y, E, Z, X, C), AXES)
    seq = ("e", "zl", "x", "core")
    columns = P(None, seq + ("sect",))
    return jax.shard_map(
        local,
        mesh=fine,
        in_specs=(P(seq, None), P(seq, None), P(), columns, columns, columns),
        out_specs=(columns, P(seq, None), P()),
        check_vma=False,
    )
```

```python
import jax
import jax.numpy as jnp
from jax import lax
from jax.experimental import pallas as pl
from jax.experimental.pallas import tpu as pltpu
from jax.sharding import Mesh, PartitionSpec as P

AXES = ("sect", "e", "zl", "xh", "xl", "core")
HBM = pltpu.MemorySpace.HBM
bf16, f32, i32 = jnp.bfloat16, jnp.float32, jnp.int32
Y, E, Z, X, C = 4, 8, 2, 2, 2
M = Z * X
MOST = 3
GROUP = E * C * MOST
BLOCK = GROUP + 8
LIMIT = 48 * 1024 * 1024
MOST_VMEM = 60 * 1024 * 1024
LONG = pl.CostEstimate(flops=40_000_000_000, bytes_accessed=100_000_000, transcendentals=0)
LESS = pl.CostEstimate(flops=22_000_000_000, bytes_accessed=10_000_000, transcendentals=0)


def iota(shape, dim):
    return lax.broadcasted_iota(i32, shape, dim)


def split2(v):
    hi = v.astype(bf16).astype(f32)
    return hi, v - hi


def route_kernel(place_ref, routes_ref, tokens_ref, router_ref, out_ref, logits_ref):
    tok = tokens_ref.shape[0]
    piece = out_ref.shape[-1]
    sect = place_ref[0]
    logits = lax.dot_general(
        tokens_ref[...], router_ref[...], (((1,), (1,)), ((), ())), preferred_element_type=f32
    )
    logits_ref[...] = logits
    row, lane = iota((tok, E), 0), iota((tok, E), 1)
    chosen = []
    for k in range(2):
        named = jnp.zeros((tok, E), i32)
        for t in range(tok):
            named = jnp.where(row == t, routes_ref[k, t], named)
        chosen.append(jnp.sum(jnp.where(lane == named, logits, 0.0), axis=1, keepdims=True))
    top = jnp.maximum(chosen[0], chosen[1])
    a, b = jnp.exp(chosen[0] - top), jnp.exp(chosen[1] - top)
    probs = [a / (a + b), b / (a + b)]
    hi, lo = split2(probs[0] * probs[1])

    pairs = [(t, k, routes_ref[k, t], routes_ref[1 - k, t]) for t in range(tok) for k in range(2)]
    ranks = []
    for i, pair in enumerate(pairs):
        rank = jnp.int32(0)
        for j in range(i):
            rank = rank + (pairs[j][2] == pair[2]).astype(i32)
        ranks.append(rank)

    rows8, lanes8 = iota((E, 128), 0), iota((E, 128), 1)
    meta = jnp.zeros((E, 128), f32)
    for (t, k, expert, other), rank in zip(pairs, ranks):
        here = rows8 == expert
        meta = jnp.where(here & (lanes8 == rank), (other + 1).astype(f32), meta)
        for q, value in ((1, probs[k]), (2, hi), (3, lo)):
            meta = jnp.where(here & (lanes8 == q * MOST + rank), value[t : t + 1, :], meta)
    meta = jnp.concatenate([meta, jnp.zeros((E, piece - 128), f32)], axis=1)

    rows_e = iota((E, piece), 0)
    for c in range(C):
        start = pl.multiple_of((c * Y + sect) * piece, 128)
        mine = tokens_ref[:, pl.ds(start, piece)].astype(f32)
        acc = [jnp.zeros((E, piece), f32) for _ in range(MOST)]
        for (t, _, expert, _), rank in zip(pairs, ranks):
            value = jnp.broadcast_to(mine[t : t + 1, :], (E, piece))
            for r in range(MOST):
                there = rows_e == jnp.where(rank == r, expert, -1)
                acc[r] = jnp.where(there, value, acc[r])
        for e in range(E):
            rows = [v[e : e + 1] for v in (*acc, meta)]
            out_ref[e, c] = jnp.concatenate(rows, axis=0).astype(bf16)


def gather_kernel(arrived_ref, out_ref, block_ref):
    @pl.when(pl.program_id(0) == 0)
    def _():
        count = E * C
        flat = jnp.concatenate([arrived_ref[j].astype(f32) for j in range(count)], axis=0)
        flat = flat.astype(bf16)
        slot, source = iota((GROUP, 4 * count), 0), iota((GROUP, 4 * count), 1)
        pick = jnp.where(source == slot // MOST * 4 + slot % MOST, 1.0, 0.0).astype(bf16)
        block_ref[0:GROUP, :] = jnp.dot(pick, flat, preferred_element_type=f32).astype(bf16)
        pick = jnp.where(source == slot // MOST * 4 + MOST, 1.0, 0.0).astype(bf16)
        notes = jnp.dot(pick, flat[:, 0:128], preferred_element_type=f32)
        slot, lane = iota((GROUP, 128), 0), iota((GROUP, 128), 1)
        rows = []
        for q in range(4):
            column = jnp.sum(
                jnp.where(lane == q * MOST + slot % MOST, notes, 0.0), axis=1, keepdims=True
            )
            rows.append(jnp.sum(jnp.where(lane == slot, column, 0.0), axis=0, keepdims=True))
        rows.append(jnp.zeros((4, 128), f32))
        rest = jnp.zeros((8, block_ref.shape[1] - 128), f32)
        notes = jnp.concatenate([jnp.concatenate(rows, axis=0), rest], axis=1)
        block_ref[GROUP:BLOCK, :] = notes.astype(bf16)

    for i in range(M):
        out_ref[i] = block_ref[...]


def gathered_rows(rows_ref):
    return jnp.concatenate([rows_ref[i, 0:GROUP, :] for i in range(M)], axis=0)


def side(refs):
    own, near, gate, up = refs[0:4], refs[4], refs[5], refs[6]
    parts = [v[...] for v in own] + [near[0], near[1], gate[0], up[0]]
    return [jnp.concatenate(parts[i : i + 2], axis=1) for i in range(0, 8, 2)]


def half_kernel(place_ref, *refs):
    for i, ref in enumerate(refs[:-1]):
        refs[-1][i] = ref[...]


def pre_kernel(place_ref, rows_ref, *refs):
    weights, (own_ref, core_ref, flat_ref) = side(refs[0:7]), refs[7:10]
    width = rows_ref.shape[2]
    for y in range(Y):
        for i in range(M):
            flat_ref[i * GROUP : (i + 1) * GROUP, y * width : (y + 1) * width] = rows_ref[
                y * M + i, 0:GROUP, :
            ]
    for out, start, part in zip(
        (own_ref, own_ref, core_ref, core_ref), (0, 256, 0, 256), weights
    ):
        out[:, start : start + 256] = jnp.dot(flat_ref[...], part, preferred_element_type=f32)


def act_kernel(
    expert_ref, own_ref, core_ref, cot_ref, far_cot_ref, rows_ref, hidden_ref, far_ref, d_ref, coef_ref
):
    slots = own_ref.shape[0]
    eye = iota((GROUP, 128), 0) == iota((GROUP, 128), 1)

    def column(q):
        parts = []
        for i in range(M):
            notes = rows_ref[i, GROUP:BLOCK, 0:128].astype(f32)
            parts.append(jnp.sum(jnp.where(eye, notes[q : q + 1], 0.0), axis=1, keepdims=True))
        return jnp.concatenate(parts, axis=0)

    other = (column(0) - 1.0).astype(i32)
    weight = column(1)
    both = column(2) + column(3)
    dp = jnp.zeros((slots, 1), f32)
    for i, (cot, out) in enumerate(((cot_ref, hidden_ref), (far_cot_ref, far_ref))):
        first = slice(i * 256, i * 256 + 128)
        second = slice(i * 256 + 128, i * 256 + 256)
        gate = own_ref[:, first] + core_ref[:, first]
        up = own_ref[:, second] + core_ref[:, second]
        sigma = jax.nn.sigmoid(gate)
        act = gate * sigma * up
        out[...] = (weight * act).astype(bf16)
        grad_out = cot[...].astype(f32)
        dp = dp + jnp.sum(grad_out * act, axis=1, keepdims=True)
        d_gate = grad_out * weight * up * sigma * (1.0 + gate * (1.0 - sigma))
        d_up = grad_out * weight * gate * sigma
        d_ref[:, first] = d_gate.astype(bf16)
        d_ref[:, second] = d_up.astype(bf16)
    hi, rest = split2(dp)
    lo, last = split2(rest)
    lane = iota((slots, 128), 1)
    d_ref[:, 512:640] = jnp.where(
        lane == 0, hi, jnp.where(lane == 1, lo, jnp.where(lane == 2, last, 0.0))
    ).astype(bf16)
    third = lane % E
    sign = jnp.where(third == expert_ref[0], 1.0, 0.0) - jnp.where(third == other, 1.0, 0.0)
    coef_ref[...] = jnp.where(lane < 3 * E, sign * both, 0.0)


def dx_kernel(place_ref, own_ref, core_ref, coef_ref, *refs):
    weights, (rows_ref, out_ref, three_ref, dp_ref) = side(refs[0:7]), refs[7:11]
    slots = own_ref.shape[0]
    rows = gathered_rows(rows_ref)
    width = rows.shape[1]

    @pl.when(pl.program_id(0) == 0)
    def _():
        def dp_of(ref):
            return jnp.sum(ref[:, 512:640].astype(f32), axis=1, keepdims=True)

        dp = dp_of(own_ref)
        coef = coef_ref[...] * (dp + dp_of(core_ref))
        hi, rest = split2(coef)
        lo, last = split2(rest)
        lane = iota((slots, 128), 1)
        three = jnp.where(lane < E, hi, jnp.where(lane < 2 * E, lo, last))
        three_ref[...] = three.T[0:32].astype(bf16)
        eye = iota((GROUP, 128), 0) == iota((GROUP, 128), 1)
        parts = []
        for i in range(M):
            for v in split2(dp[i * GROUP : (i + 1) * GROUP]):
                parts.append(jnp.sum(jnp.where(eye, v, 0.0), axis=0, keepdims=True))
        dp_ref[...] = jnp.concatenate(parts, axis=0)

    dims = (((1,), (1,)), ((), ()))
    dx = None
    for d_ref, start, part in zip(
        (own_ref, own_ref, core_ref, core_ref), (0, 256, 0, 256), weights
    ):
        d = d_ref[:, start : start + 256]
        got = lax.dot_general(d, part, dims, preferred_element_type=f32)
        dx = got if dx is None else dx + got
    got = jnp.dot(three_ref[...], rows, preferred_element_type=f32)
    router = got[0:E] + got[E : 2 * E] + got[2 * E : 3 * E]
    router_hi, router_lo = split2(router)
    for i in range(M):
        out_ref[i, 0:GROUP, :] = dx[i * GROUP : (i + 1) * GROUP].astype(bf16)
        dp_rows = jnp.concatenate(
            [dp_ref[2 * i : 2 * i + 2], jnp.zeros((2, width - 128), f32)], axis=1
        )
        meta = [router_hi[2 * i : 2 * i + 2], router_lo[2 * i : 2 * i + 2], dp_rows]
        meta = jnp.concatenate([*meta, jnp.zeros((2, width), f32)], axis=0)
        out_ref[i, GROUP:BLOCK, :] = meta.astype(bf16)


def sum_kernel(recv_ref, out_ref, acc_ref):
    step = pl.program_id(0)
    total = jnp.sum(recv_ref[...].astype(f32), axis=0)

    @pl.when(step == 0)
    def _():
        acc_ref[...] = total

    @pl.when(step != 0)
    def _():
        acc_ref[...] += total

    @pl.when(step == pl.num_programs(0) - 1)
    def _():
        meta = acc_ref[GROUP:BLOCK, :]
        router_hi, router_lo = split2(meta[0:2] + meta[2:4])
        dp_hi, dp_lo = split2(meta[4:5, 0:128] + meta[5:6, 0:128])
        dp_row = jnp.concatenate([jnp.zeros((1, 512), f32), dp_hi, dp_lo], axis=1)
        source = jnp.concatenate(
            [acc_ref[0:GROUP, :], router_hi, router_lo, dp_row, jnp.zeros((3, 768), f32)], axis=0
        ).astype(bf16)
        shape = (E * C * 8, BLOCK)
        column = iota(shape, 1)
        place, q = iota(shape, 0) // 8, iota(shape, 0) % 8
        hi, lo, dp = GROUP + place % 2, GROUP + 2 + place % 2, jnp.full(shape, GROUP + 4, i32)

        def pick_rows(cases):
            target = jnp.full(shape, -1, i32)
            for value, where in cases:
                target = jnp.where(q == value, where, target)
            return jnp.where(column == target, 1.0, 0.0).astype(bf16)

        slot = MOST * place
        first = pick_rows([(0, slot), (1, slot + 1), (2, slot + 2), (5, hi), (6, lo)])
        left = pick_rows([(3, slot), (4, slot + 2), (7, lo)])
        right = pick_rows([(3, slot + 1), (4, hi), (7, dp)])
        got = jnp.dot(first, source[:, 0:512], preferred_element_type=f32)
        tail = source[:, 512:768]
        out_ref[:, 0:256] = (
            got[:, 0:256] + jnp.dot(left, tail, preferred_element_type=f32)
        ).astype(bf16)
        out_ref[:, 256:512] = (
            got[:, 256:512] + jnp.dot(right, tail, preferred_element_type=f32)
        ).astype(bf16)


def call(kernel, grid, in_specs, out_specs, out_shape, scratch=(), limit=LIMIT):
    return pl.pallas_call(
        kernel,
        grid=grid,
        in_specs=in_specs,
        out_specs=out_specs,
        out_shape=out_shape,
        scratch_shapes=list(scratch),
        compiler_params=pltpu.CompilerParams(vmem_limit_bytes=limit),
    )


def placed(kernel, grid, in_specs, out_specs, out_shape, scratch=(), cost=None):
    return pl.pallas_call(
        kernel,
        grid_spec=pltpu.PrefetchScalarGridSpec(
            num_scalar_prefetch=1,
            grid=grid,
            in_specs=in_specs,
            out_specs=out_specs,
            scratch_shapes=list(scratch),
        ),
        out_shape=out_shape,
        compiler_params=pltpu.CompilerParams(vmem_limit_bytes=LIMIT),
        cost_estimate=cost,
    )


def whole(*shape):
    return pl.BlockSpec(shape, lambda *_: (0,) * len(shape))


def in_hbm(v):
    return pltpu.with_memory_space_constraint(v, HBM)


def a2a(v, axes):
    return lax.all_to_all(v, axes, split_axis=0, concat_axis=0, tiled=True)


def everywhere(v, count):
    return jnp.broadcast_to(v[None], (count,) + v.shape)


def swap(v):
    return lax.ppermute(v, "core", [(0, 1), (1, 0)])


def along_x(v):
    order = []
    for x in range(2 * X):
        for c in range(C):
            order.append((x * C + c, (x ^ 1 if c == 0 else 2 * X - 1 - x) * C + c))
    return lax.ppermute(v, ("xh", "xl", "core"), order)


def pick(v, index, axis):
    return lax.dynamic_index_in_dim(v, index, axis=axis, keepdims=False)


def local(tokens, routes, w_router, w_gate, w_up, cotangent):
    tok, width = tokens.shape
    half, piece = width // C, width // (C * Y)
    core, xl, sect = lax.axis_index("core"), lax.axis_index("xl"), lax.axis_index("sect")
    expert = lax.axis_index("e")
    slots = cotangent.shape[0] // 2
    sds = jax.ShapeDtypeStruct
    smem = pl.BlockSpec(memory_space=pltpu.SMEM)

    far_gate, far_up = along_x(w_gate), along_x(w_up)

    message, logits = call(
        route_kernel,
        (1,),
        [smem, smem, whole(tok, width), whole(E, width)],
        [whole(E, C, MOST + 1, piece), whole(tok, E)],
        [sds((E, C, MOST + 1, piece), bf16), sds((tok, E), f32)],
        limit=MOST_VMEM,
    )(sect.reshape(1).astype(i32), routes.T, tokens, w_router.T)
    arrived = a2a(message.reshape(E * C, MOST + 1, piece), ("e", "core"))

    place = core.reshape(1).astype(i32)

    def other_half(parts, cost=None):
        block = pl.BlockSpec((half, 128), lambda i, place: (1 - place[0], 0))
        return pl.pallas_call(
            half_kernel,
            grid_spec=pltpu.PrefetchScalarGridSpec(
                num_scalar_prefetch=1,
                grid=(1,),
                in_specs=[block] * len(parts),
                out_specs=whole(len(parts), half, 128),
            ),
            out_shape=sds((len(parts), half, 128), bf16),
            compiler_params=pltpu.CompilerParams(vmem_limit_bytes=LIMIT),
            cost_estimate=cost,
        )(place, *parts)

    near_other = other_half([w_gate, w_up])
    weights = (w_gate, w_up, far_gate, far_up, swap(near_other))
    weights += (swap(other_half([far_gate], LONG)), swap(other_half([far_up], LESS)))

    weights = [in_hbm(v) for v in weights]
    cot, _ = lax.optimization_barrier((cotangent, near_other))
    cot = cot.reshape(E, Z, X, 2, C * MOST, 128).transpose(3, 1, 2, 0, 4, 5)
    cot = cot.reshape(2, slots, 128)
    near_cot, far_cot = pick(cot, xl, 0), along_x(pick(cot, 1 - xl, 0))

    rows_spec = pl.BlockSpec((M, BLOCK, piece), lambda i: (i, 0, 0))
    gathered = call(
        gather_kernel,
        (Y,),
        [whole(E * C, MOST + 1, piece)],
        rows_spec,
        HBM((Y * M, BLOCK, piece), bf16),
        [pltpu.VMEM((BLOCK, piece), bf16)],
    )(arrived)
    rows = a2a(gathered, ("sect", "zl", "xh"))

    rows, near_cot, far_cot = lax.optimization_barrier((rows, near_cot, far_cot))

    def w_specs(rows, count):
        own = pl.BlockSpec((rows, 128), lambda i, place: (place[0] * count + i, 0))
        core = [pl.BlockSpec((n, rows, 128), lambda i, place: (0, i, 0)) for n in (2, 1, 1)]
        return [own] * 4 + core

    step_spec = pl.BlockSpec((M, BLOCK, piece), lambda i, place: (i, 0, 0))
    part = sds((slots, 512), f32)
    own, to_core = placed(
        pre_kernel,
        (1,),
        [whole(Y * M, BLOCK, piece)] + w_specs(half, 1),
        [whole(slots, 512), whole(slots, 512)],
        [part, part],
        [pltpu.VMEM((slots, half), bf16)],
    )(place, rows, *weights)
    hidden, far_hidden, d, coef = call(
        act_kernel,
        (1,),
        [smem]
        + [whole(slots, 512)] * 2
        + [whole(slots, 128)] * 2
        + [whole(M, BLOCK, piece)],
        [whole(slots, 128), whole(slots, 128), whole(slots, 640), whole(slots, 128)],
        [sds((slots, 128), bf16)] * 2 + [sds((slots, 640), bf16), sds((slots, 128), f32)],
    )(expert.reshape(1).astype(i32), own, swap(to_core), near_cot, far_cot, rows)

    back = placed(
        dx_kernel,
        (Y,),
        [whole(slots, 640)] * 2 + [whole(slots, 128)] + w_specs(piece, Y) + [step_spec],
        step_spec,
        HBM((Y * M, BLOCK, piece), bf16),
        [pltpu.VMEM((32, slots), bf16), pltpu.VMEM((2 * M, 128), f32)],
    )(place, d, swap(d), coef, *weights, rows)

    hidden_back = along_x(far_hidden)
    back = a2a(back, ("sect", "zl", "xh"))
    summed = call(
        sum_kernel,
        (Y,),
        [rows_spec],
        whole(E * C * 8, 512),
        sds((E * C * 8, 512), bf16),
        [pltpu.VMEM((BLOCK, piece), f32)],
    )(back)
    pairs = routes.reshape(-1)
    count = tok * 2
    same = pairs[:, None] == pairs[None, :]
    earlier = jnp.arange(count)[None, :] < jnp.arange(count)[:, None]
    ranks = jnp.sum((same & earlier).astype(i32), axis=1)
    places = pairs * MOST + ranks
    select = (places[None, :] == jnp.arange(E * MOST, dtype=i32)[:, None]).astype(f32)
    spread = jnp.sum(select.reshape(E * MOST, tok, 2), axis=2).astype(bf16)
    spread = spread.T.reshape(tok, E, MOST)
    choose = (routes[:, :, None] == jnp.arange(E, dtype=i32)[None, None, :]).astype(f32)
    probs = jax.nn.softmax(jnp.sum(choose * logits[:, None, :], axis=2), axis=1)
    w_mine = pick(w_router.reshape(C, Y, piece, E), sect, 1).astype(f32)

    summed, hidden_back, select, spread, choose, probs, w_mine = lax.optimization_barrier(
        (summed, hidden_back, select, spread, choose, probs, w_mine)
    )
    home = a2a(summed.reshape(E * C, 8, 512), ("e", "core"))
    home = home.reshape(E, C, 8, 512)

    mine = xl == jnp.arange(2)[:, None, None]
    hidden = jnp.where(mine, hidden[None], hidden_back[None])
    hidden = hidden.reshape(2, Z, X, E, C * MOST, 128).transpose(3, 1, 2, 0, 4, 5)
    hidden = hidden.reshape(2 * slots, 128)

    router_parts = jnp.concatenate(
        [
            home[:, :, 5, :].astype(f32) + home[:, :, 6, :].astype(f32),
            home[:, :, 4, 256:512].astype(f32) + home[:, :, 7, 0:256].astype(f32),
        ],
        axis=2,
    )
    router = jnp.sum(router_parts, axis=0).reshape(C * piece // 128, 128)
    router = a2a(everywhere(router, 2 * M * C), ("xl", "zl", "xh", "core"))

    tails = [home[:, :, 3, 0:256], home[:, :, 3, 256:512], home[:, :, 4, 0:256]]
    main = jnp.concatenate([home[:, :, 0:3, :], jnp.stack(tails, axis=2)], axis=3)
    token_dx = jnp.einsum("ter,ecrd->tcd", spread, main, preferred_element_type=f32)
    dp = jnp.sum(home[:, :, 7, 256:512].astype(f32), axis=1)
    dp = dp[:, 0:128] + dp[:, 128:256]
    dp = lax.dynamic_slice_in_dim(dp, (expert * C + core) * MOST, MOST, 1).reshape(E * MOST)
    pair_dp = jnp.sum(select * dp[:, None], axis=0).reshape(tok, 2)
    mean_dp = jnp.sum(probs * pair_dp, axis=1, keepdims=True)
    d_pick = probs * (pair_dp - mean_dp)
    d_logits = jnp.sum(choose * d_pick[:, :, None], axis=1)
    router_dx = jnp.einsum("te,cde->tcd", d_logits, w_mine, precision=lax.Precision.HIGHEST)
    grad_tokens = (token_dx + router_dx).astype(bf16).reshape(tok, C * piece)

    router = jnp.sum(router.reshape(2, E, C * piece), axis=0)
    hi = lax.reduce_precision(router, 8, 7)
    parts = [grad_tokens, hi.astype(bf16), (router - hi).astype(bf16)]
    got = a2a(everywhere(jnp.concatenate(parts, axis=0), Y), ("sect",))

    def whole_width(v):
        return v.reshape(Y, -1, C, piece).transpose(1, 2, 0, 3).reshape(-1, width)

    grad_tokens = whole_width(got[:, 0:tok])
    parts = got[:, tok:].astype(f32)
    grad_router = whole_width(parts[:, 0:E] + parts[:, E:])
    return hidden, grad_tokens, grad_router.T


def solution(mesh):
    fine = Mesh(mesh.devices.reshape(Y, E, Z, X, 2, C), AXES)
    seq = ("e", "zl", "xh", "xl", "core")
    columns = P(None, seq + ("sect",))
    return jax.shard_map(
        local,
        mesh=fine,
        in_specs=(P(seq, None), P(seq, None), P(), columns, columns, columns),
        out_specs=(columns, P(seq, None), P()),
        check_vma=False,
    )
```

```python
import jax
import jax.numpy as jnp
from jax import lax
from jax.experimental import pallas as pl
from jax.experimental.pallas import tpu as pltpu
from jax.sharding import Mesh, PartitionSpec as P

AXES = ("sect", "e", "zl", "xh", "xl", "core")
HBM = pltpu.MemorySpace.HBM
bf16, f32, i32 = jnp.bfloat16, jnp.float32, jnp.int32
Y, E, Z, X, C = 4, 8, 2, 2, 2
M = Z * X
MOST = 3
GROUP = E * C * MOST
BLOCK = GROUP + 8
LIMIT = 48 * 1024 * 1024
MOST_VMEM = 60 * 1024 * 1024
LONG = pl.CostEstimate(flops=40_000_000_000, bytes_accessed=100_000_000, transcendentals=0)
LESS = pl.CostEstimate(flops=22_000_000_000, bytes_accessed=10_000_000, transcendentals=0)


def iota(shape, dim):
    return lax.broadcasted_iota(i32, shape, dim)


def split2(v):
    hi = v.astype(bf16).astype(f32)
    return hi, v - hi


def route_kernel(place_ref, routes_ref, tokens_ref, router_ref, out_ref, logits_ref):
    tok = tokens_ref.shape[0]
    piece = out_ref.shape[-1]
    sect = place_ref[0]
    logits = lax.dot_general(
        tokens_ref[...], router_ref[...], (((1,), (1,)), ((), ())), preferred_element_type=f32
    )
    logits_ref[...] = logits
    row, lane = iota((tok, E), 0), iota((tok, E), 1)
    chosen = []
    for k in range(2):
        named = jnp.zeros((tok, E), i32)
        for t in range(tok):
            named = jnp.where(row == t, routes_ref[k, t], named)
        chosen.append(jnp.sum(jnp.where(lane == named, logits, 0.0), axis=1, keepdims=True))
    top = jnp.maximum(chosen[0], chosen[1])
    a, b = jnp.exp(chosen[0] - top), jnp.exp(chosen[1] - top)
    probs = [a / (a + b), b / (a + b)]
    hi, lo = split2(probs[0] * probs[1])

    pairs = [(t, k, routes_ref[k, t], routes_ref[1 - k, t]) for t in range(tok) for k in range(2)]
    ranks = []
    for i, pair in enumerate(pairs):
        rank = jnp.int32(0)
        for j in range(i):
            rank = rank + (pairs[j][2] == pair[2]).astype(i32)
        ranks.append(rank)

    rows8, lanes8 = iota((E, 128), 0), iota((E, 128), 1)
    meta = jnp.zeros((E, 128), f32)
    for (t, k, expert, other), rank in zip(pairs, ranks):
        here = rows8 == expert
        meta = jnp.where(here & (lanes8 == rank), (other + 1).astype(f32), meta)
        for q, value in ((1, probs[k]), (2, hi), (3, lo)):
            meta = jnp.where(here & (lanes8 == q * MOST + rank), value[t : t + 1, :], meta)
    meta = jnp.concatenate([meta, jnp.zeros((E, piece - 128), f32)], axis=1)

    rows_e = iota((E, piece), 0)
    for c in range(C):
        start = pl.multiple_of((c * Y + sect) * piece, 128)
        mine = tokens_ref[:, pl.ds(start, piece)].astype(f32)
        acc = [jnp.zeros((E, piece), f32) for _ in range(MOST)]
        for (t, _, expert, _), rank in zip(pairs, ranks):
            value = jnp.broadcast_to(mine[t : t + 1, :], (E, piece))
            for r in range(MOST):
                there = rows_e == jnp.where(rank == r, expert, -1)
                acc[r] = jnp.where(there, value, acc[r])
        for e in range(E):
            rows = [v[e : e + 1] for v in (*acc, meta)]
            out_ref[e, c] = jnp.concatenate(rows, axis=0).astype(bf16)


def gather_kernel(arrived_ref, out_ref, block_ref):
    @pl.when(pl.program_id(0) == 0)
    def _():
        count = E * C
        flat = jnp.concatenate([arrived_ref[j].astype(f32) for j in range(count)], axis=0)
        flat = flat.astype(bf16)
        slot, source = iota((GROUP, 4 * count), 0), iota((GROUP, 4 * count), 1)
        pick = jnp.where(source == slot // MOST * 4 + slot % MOST, 1.0, 0.0).astype(bf16)
        block_ref[0:GROUP, :] = jnp.dot(pick, flat, preferred_element_type=f32).astype(bf16)
        pick = jnp.where(source == slot // MOST * 4 + MOST, 1.0, 0.0).astype(bf16)
        notes = jnp.dot(pick, flat[:, 0:128], preferred_element_type=f32)
        slot, lane = iota((GROUP, 128), 0), iota((GROUP, 128), 1)
        rows = []
        for q in range(4):
            column = jnp.sum(
                jnp.where(lane == q * MOST + slot % MOST, notes, 0.0), axis=1, keepdims=True
            )
            rows.append(jnp.sum(jnp.where(lane == slot, column, 0.0), axis=0, keepdims=True))
        rows.append(jnp.zeros((4, 128), f32))
        rest = jnp.zeros((8, block_ref.shape[1] - 128), f32)
        notes = jnp.concatenate([jnp.concatenate(rows, axis=0), rest], axis=1)
        block_ref[GROUP:BLOCK, :] = notes.astype(bf16)

    for i in range(M):
        out_ref[i] = block_ref[...]


def gathered_rows(rows_ref):
    return jnp.concatenate([rows_ref[i, 0:GROUP, :] for i in range(M)], axis=0)


def side(refs):
    own, near, gate, up = refs[0:4], refs[4], refs[5], refs[6]
    parts = [v[...] for v in own] + [near[0], near[1], gate[0], up[0]]
    return [jnp.concatenate(parts[i : i + 2], axis=1) for i in range(0, 8, 2)]


def half_kernel(place_ref, *refs):
    for i, ref in enumerate(refs[:-1]):
        refs[-1][i] = ref[...]


def pre_kernel(place_ref, rows_ref, *refs):
    weights, (own_ref, core_ref, flat_ref) = side(refs[0:7]), refs[7:10]
    width = rows_ref.shape[2]
    for y in range(Y):
        for i in range(M):
            flat_ref[i * GROUP : (i + 1) * GROUP, y * width : (y + 1) * width] = rows_ref[
                y * M + i, 0:GROUP, :
            ]
    for out, start, part in zip(
        (own_ref, own_ref, core_ref, core_ref), (0, 256, 0, 256), weights
    ):
        out[:, start : start + 256] = jnp.dot(flat_ref[...], part, preferred_element_type=f32)


def act_kernel(
    expert_ref, own_ref, core_ref, cot_ref, far_cot_ref, rows_ref, hidden_ref, far_ref, d_ref, coef_ref
):
    slots = own_ref.shape[0]
    eye = iota((GROUP, 128), 0) == iota((GROUP, 128), 1)

    def column(q):
        parts = []
        for i in range(M):
            notes = rows_ref[i, GROUP:BLOCK, 0:128].astype(f32)
            parts.append(jnp.sum(jnp.where(eye, notes[q : q + 1], 0.0), axis=1, keepdims=True))
        return jnp.concatenate(parts, axis=0)

    other = (column(0) - 1.0).astype(i32)
    weight = column(1)
    both = column(2) + column(3)
    dp = jnp.zeros((slots, 1), f32)
    for i, (cot, out) in enumerate(((cot_ref, hidden_ref), (far_cot_ref, far_ref))):
        first = slice(i * 256, i * 256 + 128)
        second = slice(i * 256 + 128, i * 256 + 256)
        gate = own_ref[:, first] + core_ref[:, first]
        up = own_ref[:, second] + core_ref[:, second]
        sigma = jax.nn.sigmoid(gate)
        act = gate * sigma * up
        out[...] = (weight * act).astype(bf16)
        grad_out = cot[...].astype(f32)
        dp = dp + jnp.sum(grad_out * act, axis=1, keepdims=True)
        d_gate = grad_out * weight * up * sigma * (1.0 + gate * (1.0 - sigma))
        d_up = grad_out * weight * gate * sigma
        d_ref[:, first] = d_gate.astype(bf16)
        d_ref[:, second] = d_up.astype(bf16)
    hi, rest = split2(dp)
    lo, last = split2(rest)
    lane = iota((slots, 128), 1)
    d_ref[:, 512:640] = jnp.where(
        lane == 0, hi, jnp.where(lane == 1, lo, jnp.where(lane == 2, last, 0.0))
    ).astype(bf16)
    third = lane % E
    sign = jnp.where(third == expert_ref[0], 1.0, 0.0) - jnp.where(third == other, 1.0, 0.0)
    coef_ref[...] = jnp.where(lane < 3 * E, sign * both, 0.0)


def dx_kernel(place_ref, own_ref, core_ref, coef_ref, *refs):
    weights, (rows_ref, out_ref, three_ref, dp_ref) = side(refs[0:7]), refs[7:11]
    slots = own_ref.shape[0]
    rows = gathered_rows(rows_ref)
    width = rows.shape[1]

    @pl.when(pl.program_id(0) == 0)
    def _():
        def dp_of(ref):
            return jnp.sum(ref[:, 512:640].astype(f32), axis=1, keepdims=True)

        dp = dp_of(own_ref)
        coef = coef_ref[...] * (dp + dp_of(core_ref))
        hi, rest = split2(coef)
        lo, last = split2(rest)
        lane = iota((slots, 128), 1)
        three = jnp.where(lane < E, hi, jnp.where(lane < 2 * E, lo, last))
        three_ref[...] = three.T[0:32].astype(bf16)
        eye = iota((GROUP, 128), 0) == iota((GROUP, 128), 1)
        parts = []
        for i in range(M):
            for v in split2(dp[i * GROUP : (i + 1) * GROUP]):
                parts.append(jnp.sum(jnp.where(eye, v, 0.0), axis=0, keepdims=True))
        dp_ref[...] = jnp.concatenate(parts, axis=0)

    dims = (((1,), (1,)), ((), ()))
    dx = None
    for d_ref, start, part in zip(
        (own_ref, own_ref, core_ref, core_ref), (0, 256, 0, 256), weights
    ):
        d = d_ref[:, start : start + 256]
        got = lax.dot_general(d, part, dims, preferred_element_type=f32)
        dx = got if dx is None else dx + got
    got = jnp.dot(three_ref[...], rows, preferred_element_type=f32)
    router = got[0:E] + got[E : 2 * E] + got[2 * E : 3 * E]
    router_hi, router_lo = split2(router)
    for i in range(M):
        out_ref[i, 0:GROUP, :] = dx[i * GROUP : (i + 1) * GROUP].astype(bf16)
        dp_rows = jnp.concatenate(
            [dp_ref[2 * i : 2 * i + 2], jnp.zeros((2, width - 128), f32)], axis=1
        )
        meta = [router_hi[2 * i : 2 * i + 2], router_lo[2 * i : 2 * i + 2], dp_rows]
        meta = jnp.concatenate([*meta, jnp.zeros((2, width), f32)], axis=0)
        out_ref[i, GROUP:BLOCK, :] = meta.astype(bf16)


def sum_kernel(recv_ref, out_ref, acc_ref):
    step = pl.program_id(0)
    total = jnp.sum(recv_ref[...].astype(f32), axis=0)

    @pl.when(step == 0)
    def _():
        acc_ref[...] = total

    @pl.when(step != 0)
    def _():
        acc_ref[...] += total

    @pl.when(step == pl.num_programs(0) - 1)
    def _():
        meta = acc_ref[GROUP:BLOCK, :]
        router_hi, router_lo = split2(meta[0:2] + meta[2:4])
        dp_hi, dp_lo = split2(meta[4:5, 0:128] + meta[5:6, 0:128])
        dp_row = jnp.concatenate([jnp.zeros((1, 512), f32), dp_hi, dp_lo], axis=1)
        source = jnp.concatenate(
            [acc_ref[0:GROUP, :], router_hi, router_lo, dp_row, jnp.zeros((3, 768), f32)], axis=0
        ).astype(bf16)
        shape = (E * C * 8, BLOCK)
        column = iota(shape, 1)
        place, q = iota(shape, 0) // 8, iota(shape, 0) % 8
        hi, lo, dp = GROUP + place % 2, GROUP + 2 + place % 2, jnp.full(shape, GROUP + 4, i32)

        def pick_rows(cases):
            target = jnp.full(shape, -1, i32)
            for value, where in cases:
                target = jnp.where(q == value, where, target)
            return jnp.where(column == target, 1.0, 0.0).astype(bf16)

        slot = MOST * place
        first = pick_rows([(0, slot), (1, slot + 1), (2, slot + 2), (5, hi), (6, lo)])
        left = pick_rows([(3, slot), (4, slot + 2), (7, lo)])
        right = pick_rows([(3, slot + 1), (4, hi), (7, dp)])
        got = jnp.dot(first, source[:, 0:512], preferred_element_type=f32)
        tail = source[:, 512:768]
        out_ref[:, 0:256] = (
            got[:, 0:256] + jnp.dot(left, tail, preferred_element_type=f32)
        ).astype(bf16)
        out_ref[:, 256:512] = (
            got[:, 256:512] + jnp.dot(right, tail, preferred_element_type=f32)
        ).astype(bf16)


def router_kernel(home_ref, out_ref):
    rows = []
    for c in range(C):
        total = home_ref[c].astype(f32)
        for e in range(1, E):
            total = total + home_ref[e * C + c].astype(f32)
        rest = total[4:5, 256:512] + total[7:8, 0:256]
        rows.append(jnp.concatenate([total[5:6] + total[6:7], rest], axis=1))
    rows = jnp.concatenate(rows, axis=0)
    for i in range(out_ref.shape[0]):
        out_ref[i] = rows


def pack_kernel(tokens_ref, router_ref, out_ref):
    piece = router_ref.shape[2]
    for c in range(C):
        part = slice(c * piece, (c + 1) * piece)
        total = router_ref[0:E, c, :] + router_ref[E : 2 * E, c, :]
        hi, lo = split2(total)
        block = jnp.concatenate([tokens_ref[:, part].astype(f32), hi, lo], axis=0).astype(bf16)
        for y in range(Y):
            out_ref[y, :, part] = block


def last_kernel(got_ref, tokens_ref, router_ref):
    tok = tokens_ref.shape[0]
    piece = got_ref.shape[2] // C
    for y in range(Y):
        for c in range(C):
            block = got_ref[y, :, c * piece : (c + 1) * piece].astype(f32)
            part = slice((c * Y + y) * piece, (c * Y + y + 1) * piece)
            tokens_ref[:, part] = block[0:tok].astype(bf16)
            router_ref[:, part] = block[tok : tok + E] + block[tok + E :]


def call(kernel, grid, in_specs, out_specs, out_shape, scratch=(), limit=LIMIT):
    return pl.pallas_call(
        kernel,
        grid=grid,
        in_specs=in_specs,
        out_specs=out_specs,
        out_shape=out_shape,
        scratch_shapes=list(scratch),
        compiler_params=pltpu.CompilerParams(vmem_limit_bytes=limit),
    )


def placed(kernel, grid, in_specs, out_specs, out_shape, scratch=(), cost=None):
    return pl.pallas_call(
        kernel,
        grid_spec=pltpu.PrefetchScalarGridSpec(
            num_scalar_prefetch=1,
            grid=grid,
            in_specs=in_specs,
            out_specs=out_specs,
            scratch_shapes=list(scratch),
        ),
        out_shape=out_shape,
        compiler_params=pltpu.CompilerParams(vmem_limit_bytes=LIMIT),
        cost_estimate=cost,
    )


def whole(*shape):
    return pl.BlockSpec(shape, lambda *_: (0,) * len(shape))


def in_hbm(v):
    return pltpu.with_memory_space_constraint(v, HBM)


def a2a(v, axes):
    return lax.all_to_all(v, axes, split_axis=0, concat_axis=0, tiled=True)


def everywhere(v, count):
    return jnp.broadcast_to(v[None], (count,) + v.shape)


def swap(v):
    return lax.ppermute(v, "core", [(0, 1), (1, 0)])


def along_x(v):
    order = []
    for x in range(2 * X):
        for c in range(C):
            order.append((x * C + c, (x ^ 1 if c == 0 else 2 * X - 1 - x) * C + c))
    return lax.ppermute(v, ("xh", "xl", "core"), order)


def pick(v, index, axis):
    return lax.dynamic_index_in_dim(v, index, axis=axis, keepdims=False)


def local(tokens, routes, w_router, w_gate, w_up, cotangent):
    tok, width = tokens.shape
    half, piece = width // C, width // (C * Y)
    core, xl, sect = lax.axis_index("core"), lax.axis_index("xl"), lax.axis_index("sect")
    expert = lax.axis_index("e")
    slots = cotangent.shape[0] // 2
    sds = jax.ShapeDtypeStruct
    smem = pl.BlockSpec(memory_space=pltpu.SMEM)

    far_gate, far_up = along_x(w_gate), along_x(w_up)

    message, logits = call(
        route_kernel,
        (1,),
        [smem, smem, whole(tok, width), whole(E, width)],
        [whole(E, C, MOST + 1, piece), whole(tok, E)],
        [sds((E, C, MOST + 1, piece), bf16), sds((tok, E), f32)],
        limit=MOST_VMEM,
    )(sect.reshape(1).astype(i32), routes.T, tokens, w_router.T)
    arrived = a2a(message.reshape(E * C, MOST + 1, piece), ("e", "core"))

    place = core.reshape(1).astype(i32)

    def other_half(parts, cost=None):
        block = pl.BlockSpec((half, 128), lambda i, place: (1 - place[0], 0))
        return pl.pallas_call(
            half_kernel,
            grid_spec=pltpu.PrefetchScalarGridSpec(
                num_scalar_prefetch=1,
                grid=(1,),
                in_specs=[block] * len(parts),
                out_specs=whole(len(parts), half, 128),
            ),
            out_shape=sds((len(parts), half, 128), bf16),
            compiler_params=pltpu.CompilerParams(vmem_limit_bytes=LIMIT),
            cost_estimate=cost,
        )(place, *parts)

    near_other = other_half([w_gate, w_up])
    weights = (w_gate, w_up, far_gate, far_up, swap(near_other))
    weights += (swap(other_half([far_gate], LONG)), swap(other_half([far_up], LESS)))

    weights = [in_hbm(v) for v in weights]
    cot, _ = lax.optimization_barrier((cotangent, near_other))
    cot = cot.reshape(E, Z, X, 2, C * MOST, 128).transpose(3, 1, 2, 0, 4, 5)
    cot = cot.reshape(2, slots, 128)
    near_cot, far_cot = pick(cot, xl, 0), along_x(pick(cot, 1 - xl, 0))

    rows_spec = pl.BlockSpec((M, BLOCK, piece), lambda i: (i, 0, 0))
    gathered = call(
        gather_kernel,
        (Y,),
        [whole(E * C, MOST + 1, piece)],
        rows_spec,
        HBM((Y * M, BLOCK, piece), bf16),
        [pltpu.VMEM((BLOCK, piece), bf16)],
    )(arrived)
    rows = a2a(gathered, ("sect", "zl", "xh"))

    rows, near_cot, far_cot = lax.optimization_barrier((rows, near_cot, far_cot))

    def w_specs(rows, count):
        own = pl.BlockSpec((rows, 128), lambda i, place: (place[0] * count + i, 0))
        core = [pl.BlockSpec((n, rows, 128), lambda i, place: (0, i, 0)) for n in (2, 1, 1)]
        return [own] * 4 + core

    step_spec = pl.BlockSpec((M, BLOCK, piece), lambda i, place: (i, 0, 0))
    part = sds((slots, 512), f32)
    own, to_core = placed(
        pre_kernel,
        (1,),
        [whole(Y * M, BLOCK, piece)] + w_specs(half, 1),
        [whole(slots, 512), whole(slots, 512)],
        [part, part],
        [pltpu.VMEM((slots, half), bf16)],
    )(place, rows, *weights)
    hidden, far_hidden, d, coef = call(
        act_kernel,
        (1,),
        [smem]
        + [whole(slots, 512)] * 2
        + [whole(slots, 128)] * 2
        + [whole(M, BLOCK, piece)],
        [whole(slots, 128), whole(slots, 128), whole(slots, 640), whole(slots, 128)],
        [sds((slots, 128), bf16)] * 2 + [sds((slots, 640), bf16), sds((slots, 128), f32)],
    )(expert.reshape(1).astype(i32), own, swap(to_core), near_cot, far_cot, rows)

    back = placed(
        dx_kernel,
        (Y,),
        [whole(slots, 640)] * 2 + [whole(slots, 128)] + w_specs(piece, Y) + [step_spec],
        step_spec,
        HBM((Y * M, BLOCK, piece), bf16),
        [pltpu.VMEM((32, slots), bf16), pltpu.VMEM((2 * M, 128), f32)],
    )(place, d, swap(d), coef, *weights, rows)

    hidden_back = along_x(far_hidden)
    back = a2a(back, ("sect", "zl", "xh"))
    summed = call(
        sum_kernel,
        (Y,),
        [rows_spec],
        whole(E * C * 8, 512),
        sds((E * C * 8, 512), bf16),
        [pltpu.VMEM((BLOCK, piece), f32)],
    )(back)
    pairs = routes.reshape(-1)
    count = tok * 2
    same = pairs[:, None] == pairs[None, :]
    earlier = jnp.arange(count)[None, :] < jnp.arange(count)[:, None]
    ranks = jnp.sum((same & earlier).astype(i32), axis=1)
    places = pairs * MOST + ranks
    select = (places[None, :] == jnp.arange(E * MOST, dtype=i32)[:, None]).astype(f32)
    spread = jnp.sum(select.reshape(E * MOST, tok, 2), axis=2).astype(bf16)
    spread = spread.T.reshape(tok, E, MOST)
    choose = (routes[:, :, None] == jnp.arange(E, dtype=i32)[None, None, :]).astype(f32)
    probs = jax.nn.softmax(jnp.sum(choose * logits[:, None, :], axis=2), axis=1)
    w_mine = pick(w_router.reshape(C, Y, piece, E), sect, 1).astype(f32)

    summed, hidden_back, select, spread, choose, probs, w_mine = lax.optimization_barrier(
        (summed, hidden_back, select, spread, choose, probs, w_mine)
    )
    home = a2a(summed.reshape(E * C, 8, 512), ("e", "core"))
    home = home.reshape(E, C, 8, 512)

    mine = xl == jnp.arange(2)[:, None, None]
    hidden = jnp.where(mine, hidden[None], hidden_back[None])
    hidden = hidden.reshape(2, Z, X, E, C * MOST, 128).transpose(3, 1, 2, 0, 4, 5)
    hidden = hidden.reshape(2 * slots, 128)

    router = call(
        router_kernel,
        (1,),
        [whole(E * C, 8, 512)],
        whole(2 * M * C, C, piece),
        sds((2 * M * C, C, piece), f32),
    )(home.reshape(E * C, 8, 512))
    router = a2a(router, ("xl", "zl", "xh", "core"))

    tails = [home[:, :, 3, 0:256], home[:, :, 3, 256:512], home[:, :, 4, 0:256]]
    main = jnp.concatenate([home[:, :, 0:3, :], jnp.stack(tails, axis=2)], axis=3)
    token_dx = jnp.einsum("ter,ecrd->tcd", spread, main, preferred_element_type=f32)
    dp = jnp.sum(home[:, :, 7, 256:512].astype(f32), axis=1)
    dp = dp[:, 0:128] + dp[:, 128:256]
    dp = lax.dynamic_slice_in_dim(dp, (expert * C + core) * MOST, MOST, 1).reshape(E * MOST)
    pair_dp = jnp.sum(select * dp[:, None], axis=0).reshape(tok, 2)
    mean_dp = jnp.sum(probs * pair_dp, axis=1, keepdims=True)
    d_pick = probs * (pair_dp - mean_dp)
    d_logits = jnp.sum(choose * d_pick[:, :, None], axis=1)
    router_dx = jnp.einsum("te,cde->tcd", d_logits, w_mine, precision=lax.Precision.HIGHEST)
    grad_tokens = (token_dx + router_dx).astype(bf16).reshape(tok, C * piece)

    packed = call(
        pack_kernel,
        (1,),
        [whole(tok, C * piece), whole(2 * E, C, piece)],
        whole(Y, tok + 2 * E, C * piece),
        sds((Y, tok + 2 * E, C * piece), bf16),
    )(grad_tokens, router)
    grad_tokens, grad_router = call(
        last_kernel,
        (1,),
        [whole(Y, tok + 2 * E, C * piece)],
        [whole(tok, width), whole(E, width)],
        [sds((tok, width), bf16), sds((E, width), f32)],
    )(a2a(packed, ("sect",)))
    return hidden, grad_tokens, grad_router.T


def solution(mesh):
    fine = Mesh(mesh.devices.reshape(Y, E, Z, X, 2, C), AXES)
    seq = ("e", "zl", "xh", "xl", "core")
    columns = P(None, seq + ("sect",))
    return jax.shard_map(
        local,
        mesh=fine,
        in_specs=(P(seq, None), P(seq, None), P(), columns, columns, columns),
        out_specs=(columns, P(seq, None), P()),
        check_vma=False,
    )
```

```python
import jax
import jax.numpy as jnp
from jax import lax
from jax.experimental import pallas as pl
from jax.experimental.pallas import tpu as pltpu
from jax.sharding import Mesh, PartitionSpec as P

AXES = ("sect", "e", "zl", "xh", "xl", "core")
HBM = pltpu.MemorySpace.HBM
bf16, f32, i32 = jnp.bfloat16, jnp.float32, jnp.int32
Y, E, Z, X, C = 4, 8, 2, 2, 2
M = Z * X
MOST = 3
GROUP = E * C * MOST
BLOCK = GROUP + 8
LIMIT = 48 * 1024 * 1024
MOST_VMEM = 60 * 1024 * 1024
LONG = pl.CostEstimate(flops=40_000_000_000, bytes_accessed=100_000_000, transcendentals=0)
LESS = pl.CostEstimate(flops=22_000_000_000, bytes_accessed=10_000_000, transcendentals=0)


def iota(shape, dim):
    return lax.broadcasted_iota(i32, shape, dim)


def split2(v):
    hi = v.astype(bf16).astype(f32)
    return hi, v - hi


def route_kernel(place_ref, routes_ref, tokens_ref, router_ref, out_ref, logits_ref):
    tok = tokens_ref.shape[0]
    piece = out_ref.shape[-1]
    sect = place_ref[0]
    logits = lax.dot_general(
        tokens_ref[...], router_ref[...], (((1,), (1,)), ((), ())), preferred_element_type=f32
    )
    logits_ref[...] = logits
    row, lane = iota((tok, E), 0), iota((tok, E), 1)
    chosen = []
    for k in range(2):
        named = jnp.zeros((tok, E), i32)
        for t in range(tok):
            named = jnp.where(row == t, routes_ref[k, t], named)
        chosen.append(jnp.sum(jnp.where(lane == named, logits, 0.0), axis=1, keepdims=True))
    top = jnp.maximum(chosen[0], chosen[1])
    a, b = jnp.exp(chosen[0] - top), jnp.exp(chosen[1] - top)
    probs = [a / (a + b), b / (a + b)]
    hi, lo = split2(probs[0] * probs[1])

    pairs = [(t, k, routes_ref[k, t], routes_ref[1 - k, t]) for t in range(tok) for k in range(2)]
    ranks = []
    for i, pair in enumerate(pairs):
        rank = jnp.int32(0)
        for j in range(i):
            rank = rank + (pairs[j][2] == pair[2]).astype(i32)
        ranks.append(rank)

    rows8, lanes8 = iota((E, 128), 0), iota((E, 128), 1)
    meta = jnp.zeros((E, 128), f32)
    for (t, k, expert, other), rank in zip(pairs, ranks):
        here = rows8 == expert
        meta = jnp.where(here & (lanes8 == rank), (other + 1).astype(f32), meta)
        for q, value in ((1, probs[k]), (2, hi), (3, lo)):
            meta = jnp.where(here & (lanes8 == q * MOST + rank), value[t : t + 1, :], meta)
    meta = jnp.concatenate([meta, jnp.zeros((E, piece - 128), f32)], axis=1)

    rows_e = iota((E, piece), 0)
    for c in range(C):
        start = pl.multiple_of((c * Y + sect) * piece, 128)
        mine = tokens_ref[:, pl.ds(start, piece)].astype(f32)
        acc = [jnp.zeros((E, piece), f32) for _ in range(MOST)]
        for (t, _, expert, _), rank in zip(pairs, ranks):
            value = jnp.broadcast_to(mine[t : t + 1, :], (E, piece))
            for r in range(MOST):
                there = rows_e == jnp.where(rank == r, expert, -1)
                acc[r] = jnp.where(there, value, acc[r])
        for e in range(E):
            rows = [v[e : e + 1] for v in (*acc, meta)]
            out_ref[e, c] = jnp.concatenate(rows, axis=0).astype(bf16)


def gather_kernel(arrived_ref, out_ref, block_ref):
    @pl.when(pl.program_id(0) == 0)
    def _():
        count = E * C
        flat = jnp.concatenate([arrived_ref[j].astype(f32) for j in range(count)], axis=0)
        flat = flat.astype(bf16)
        slot, source = iota((GROUP, 4 * count), 0), iota((GROUP, 4 * count), 1)
        pick = jnp.where(source == slot // MOST * 4 + slot % MOST, 1.0, 0.0).astype(bf16)
        block_ref[0:GROUP, :] = jnp.dot(pick, flat, preferred_element_type=f32).astype(bf16)
        pick = jnp.where(source == slot // MOST * 4 + MOST, 1.0, 0.0).astype(bf16)
        notes = jnp.dot(pick, flat[:, 0:128], preferred_element_type=f32)
        slot, lane = iota((GROUP, 128), 0), iota((GROUP, 128), 1)
        rows = []
        for q in range(4):
            column = jnp.sum(
                jnp.where(lane == q * MOST + slot % MOST, notes, 0.0), axis=1, keepdims=True
            )
            rows.append(jnp.sum(jnp.where(lane == slot, column, 0.0), axis=0, keepdims=True))
        rows.append(jnp.zeros((4, 128), f32))
        rest = jnp.zeros((8, block_ref.shape[1] - 128), f32)
        notes = jnp.concatenate([jnp.concatenate(rows, axis=0), rest], axis=1)
        block_ref[GROUP:BLOCK, :] = notes.astype(bf16)

    for i in range(Y * M):
        out_ref[i] = block_ref[...]


def gathered_rows(rows_ref):
    return jnp.concatenate([rows_ref[i, 0:GROUP, :] for i in range(M)], axis=0)


def side(refs):
    own, near, gate, up = refs[0:4], refs[4], refs[5], refs[6]
    parts = [v[...] for v in own] + [near[0], near[1], gate[0], up[0]]
    return [jnp.concatenate(parts[i : i + 2], axis=1) for i in range(0, 8, 2)]


def half_kernel(place_ref, *refs):
    for i, ref in enumerate(refs[:-1]):
        refs[-1][i] = ref[...]


def pre_kernel(place_ref, rows_ref, *refs):
    weights, (own_ref, core_ref, flat_ref) = side(refs[0:7]), refs[7:10]
    width = rows_ref.shape[2]
    for y in range(Y):
        for i in range(M):
            flat_ref[i * GROUP : (i + 1) * GROUP, y * width : (y + 1) * width] = rows_ref[
                y * M + i, 0:GROUP, :
            ]
    for out, start, part in zip(
        (own_ref, own_ref, core_ref, core_ref), (0, 256, 0, 256), weights
    ):
        out[:, start : start + 256] = jnp.dot(flat_ref[...], part, preferred_element_type=f32)


def act_kernel(
    expert_ref, own_ref, core_ref, cot_ref, far_cot_ref, rows_ref, hidden_ref, far_ref, d_ref, coef_ref
):
    slots = own_ref.shape[0]
    eye = iota((GROUP, 128), 0) == iota((GROUP, 128), 1)

    def column(q):
        parts = []
        for i in range(M):
            notes = rows_ref[i, GROUP:BLOCK, 0:128].astype(f32)
            parts.append(jnp.sum(jnp.where(eye, notes[q : q + 1], 0.0), axis=1, keepdims=True))
        return jnp.concatenate(parts, axis=0)

    other = (column(0) - 1.0).astype(i32)
    weight = column(1)
    both = column(2) + column(3)
    dp = jnp.zeros((slots, 1), f32)
    for i, (cot, out) in enumerate(((cot_ref, hidden_ref), (far_cot_ref, far_ref))):
        first = slice(i * 256, i * 256 + 128)
        second = slice(i * 256 + 128, i * 256 + 256)
        gate = own_ref[:, first] + core_ref[:, first]
        up = own_ref[:, second] + core_ref[:, second]
        sigma = jax.nn.sigmoid(gate)
        act = gate * sigma * up
        out[...] = (weight * act).astype(bf16)
        grad_out = cot[...].astype(f32)
        dp = dp + jnp.sum(grad_out * act, axis=1, keepdims=True)
        d_gate = grad_out * weight * up * sigma * (1.0 + gate * (1.0 - sigma))
        d_up = grad_out * weight * gate * sigma
        d_ref[:, first] = d_gate.astype(bf16)
        d_ref[:, second] = d_up.astype(bf16)
    hi, rest = split2(dp)
    lo, last = split2(rest)
    lane = iota((slots, 128), 1)
    d_ref[:, 512:640] = jnp.where(
        lane == 0, hi, jnp.where(lane == 1, lo, jnp.where(lane == 2, last, 0.0))
    ).astype(bf16)
    third = lane % E
    sign = jnp.where(third == expert_ref[0], 1.0, 0.0) - jnp.where(third == other, 1.0, 0.0)
    coef_ref[...] = jnp.where(lane < 3 * E, sign * both, 0.0)


def dx_kernel(place_ref, own_ref, core_ref, coef_ref, *refs):
    weights, (rows_ref, out_ref, three_ref, dp_ref) = side(refs[0:7]), refs[7:11]
    slots = own_ref.shape[0]
    rows = gathered_rows(rows_ref)
    width = rows.shape[1]

    @pl.when(pl.program_id(0) == 0)
    def _():
        def dp_of(ref):
            return jnp.sum(ref[:, 512:640].astype(f32), axis=1, keepdims=True)

        dp = dp_of(own_ref)
        coef = coef_ref[...] * (dp + dp_of(core_ref))
        hi, rest = split2(coef)
        lo, last = split2(rest)
        lane = iota((slots, 128), 1)
        three = jnp.where(lane < E, hi, jnp.where(lane < 2 * E, lo, last))
        three_ref[...] = three.T[0:32].astype(bf16)
        eye = iota((GROUP, 128), 0) == iota((GROUP, 128), 1)
        parts = []
        for i in range(M):
            for v in split2(dp[i * GROUP : (i + 1) * GROUP]):
                parts.append(jnp.sum(jnp.where(eye, v, 0.0), axis=0, keepdims=True))
        dp_ref[...] = jnp.concatenate(parts, axis=0)

    dims = (((1,), (1,)), ((), ()))
    dx = None
    for d_ref, start, part in zip(
        (own_ref, own_ref, core_ref, core_ref), (0, 256, 0, 256), weights
    ):
        d = d_ref[:, start : start + 256]
        got = lax.dot_general(d, part, dims, preferred_element_type=f32)
        dx = got if dx is None else dx + got
    got = jnp.dot(three_ref[...], rows, preferred_element_type=f32)
    router = got[0:E] + got[E : 2 * E] + got[2 * E : 3 * E]
    router_hi, router_lo = split2(router)
    for i in range(M):
        out_ref[i, 0:GROUP, :] = dx[i * GROUP : (i + 1) * GROUP].astype(bf16)
        dp_rows = jnp.concatenate(
            [dp_ref[2 * i : 2 * i + 2], jnp.zeros((2, width - 128), f32)], axis=1
        )
        meta = [router_hi[2 * i : 2 * i + 2], router_lo[2 * i : 2 * i + 2], dp_rows]
        meta = jnp.concatenate([*meta, jnp.zeros((2, width), f32)], axis=0)
        out_ref[i, GROUP:BLOCK, :] = meta.astype(bf16)


def sum_kernel(recv_ref, out_ref, acc_ref):
    step = pl.program_id(0)
    total = jnp.sum(recv_ref[...].astype(f32), axis=0)

    @pl.when(step == 0)
    def _():
        acc_ref[...] = total

    @pl.when(step != 0)
    def _():
        acc_ref[...] += total

    @pl.when(step == pl.num_programs(0) - 1)
    def _():
        meta = acc_ref[GROUP:BLOCK, :]
        router_hi, router_lo = split2(meta[0:2] + meta[2:4])
        dp_hi, dp_lo = split2(meta[4:5, 0:128] + meta[5:6, 0:128])
        dp_row = jnp.concatenate([jnp.zeros((1, 512), f32), dp_hi, dp_lo], axis=1)
        source = jnp.concatenate(
            [acc_ref[0:GROUP, :], router_hi, router_lo, dp_row, jnp.zeros((3, 768), f32)], axis=0
        ).astype(bf16)
        shape = (E * C * 8, BLOCK)
        column = iota(shape, 1)
        place, q = iota(shape, 0) // 8, iota(shape, 0) % 8
        hi, lo, dp = GROUP + place % 2, GROUP + 2 + place % 2, jnp.full(shape, GROUP + 4, i32)

        def pick_rows(cases):
            target = jnp.full(shape, -1, i32)
            for value, where in cases:
                target = jnp.where(q == value, where, target)
            return jnp.where(column == target, 1.0, 0.0).astype(bf16)

        slot = MOST * place
        first = pick_rows([(0, slot), (1, slot + 1), (2, slot + 2), (5, hi), (6, lo)])
        left = pick_rows([(3, slot), (4, slot + 2), (7, lo)])
        right = pick_rows([(3, slot + 1), (4, hi), (7, dp)])
        got = jnp.dot(first, source[:, 0:512], preferred_element_type=f32)
        tail = source[:, 512:768]
        out_ref[:, 0:256] = (
            got[:, 0:256] + jnp.dot(left, tail, preferred_element_type=f32)
        ).astype(bf16)
        out_ref[:, 256:512] = (
            got[:, 256:512] + jnp.dot(right, tail, preferred_element_type=f32)
        ).astype(bf16)


def router_kernel(home_ref, out_ref):
    rows = []
    for c in range(C):
        total = home_ref[c].astype(f32)
        for e in range(1, E):
            total = total + home_ref[e * C + c].astype(f32)
        rest = total[4:5, 256:512] + total[7:8, 0:256]
        rows.append(jnp.concatenate([total[5:6] + total[6:7], rest], axis=1))
    rows = jnp.concatenate(rows, axis=0)
    for i in range(out_ref.shape[0]):
        out_ref[i] = rows


def pack_kernel(tokens_ref, router_ref, out_ref):
    piece = router_ref.shape[2]
    for c in range(C):
        part = slice(c * piece, (c + 1) * piece)
        total = router_ref[0:E, c, :] + router_ref[E : 2 * E, c, :]
        hi, lo = split2(total)
        block = jnp.concatenate([tokens_ref[:, part].astype(f32), hi, lo], axis=0).astype(bf16)
        for y in range(Y):
            out_ref[y, :, part] = block


def last_kernel(got_ref, tokens_ref, router_ref):
    tok = tokens_ref.shape[0]
    piece = got_ref.shape[2] // C
    for y in range(Y):
        for c in range(C):
            block = got_ref[y, :, c * piece : (c + 1) * piece].astype(f32)
            part = slice((c * Y + y) * piece, (c * Y + y + 1) * piece)
            tokens_ref[:, part] = block[0:tok].astype(bf16)
            router_ref[:, part] = block[tok : tok + E] + block[tok + E :]


def call(kernel, grid, in_specs, out_specs, out_shape, scratch=(), limit=LIMIT):
    return pl.pallas_call(
        kernel,
        grid=grid,
        in_specs=in_specs,
        out_specs=out_specs,
        out_shape=out_shape,
        scratch_shapes=list(scratch),
        compiler_params=pltpu.CompilerParams(vmem_limit_bytes=limit),
    )


def placed(kernel, grid, in_specs, out_specs, out_shape, scratch=(), cost=None):
    return pl.pallas_call(
        kernel,
        grid_spec=pltpu.PrefetchScalarGridSpec(
            num_scalar_prefetch=1,
            grid=grid,
            in_specs=in_specs,
            out_specs=out_specs,
            scratch_shapes=list(scratch),
        ),
        out_shape=out_shape,
        compiler_params=pltpu.CompilerParams(vmem_limit_bytes=LIMIT),
        cost_estimate=cost,
    )


def whole(*shape):
    return pl.BlockSpec(shape, lambda *_: (0,) * len(shape))


def in_hbm(v):
    return pltpu.with_memory_space_constraint(v, HBM)


def a2a(v, axes):
    return lax.all_to_all(v, axes, split_axis=0, concat_axis=0, tiled=True)


def everywhere(v, count):
    return jnp.broadcast_to(v[None], (count,) + v.shape)


def swap(v):
    return lax.ppermute(v, "core", [(0, 1), (1, 0)])


def along_x(v):
    order = []
    for x in range(2 * X):
        for c in range(C):
            order.append((x * C + c, (x ^ 1 if c == 0 else 2 * X - 1 - x) * C + c))
    return lax.ppermute(v, ("xh", "xl", "core"), order)


def pick(v, index, axis):
    return lax.dynamic_index_in_dim(v, index, axis=axis, keepdims=False)


def local(tokens, routes, w_router, w_gate, w_up, cotangent):
    tok, width = tokens.shape
    half, piece = width // C, width // (C * Y)
    core, xl, sect = lax.axis_index("core"), lax.axis_index("xl"), lax.axis_index("sect")
    expert = lax.axis_index("e")
    slots = cotangent.shape[0] // 2
    sds = jax.ShapeDtypeStruct
    smem = pl.BlockSpec(memory_space=pltpu.SMEM)

    far_gate, far_up = along_x(w_gate), along_x(w_up)

    message, logits = call(
        route_kernel,
        (1,),
        [smem, smem, whole(tok, width), whole(E, width)],
        [whole(E, C, MOST + 1, piece), whole(tok, E)],
        [sds((E, C, MOST + 1, piece), bf16), sds((tok, E), f32)],
        limit=MOST_VMEM,
    )(sect.reshape(1).astype(i32), routes.T, tokens, w_router.T)
    arrived = a2a(message.reshape(E * C, MOST + 1, piece), ("e", "core"))

    place = core.reshape(1).astype(i32)

    def other_half(parts, cost=None):
        block = pl.BlockSpec((half, 128), lambda i, place: (1 - place[0], 0))
        return pl.pallas_call(
            half_kernel,
            grid_spec=pltpu.PrefetchScalarGridSpec(
                num_scalar_prefetch=1,
                grid=(1,),
                in_specs=[block] * len(parts),
                out_specs=whole(len(parts), half, 128),
            ),
            out_shape=sds((len(parts), half, 128), bf16),
            compiler_params=pltpu.CompilerParams(vmem_limit_bytes=LIMIT),
            cost_estimate=cost,
        )(place, *parts)

    near_other = other_half([w_gate, w_up])
    weights = (w_gate, w_up, far_gate, far_up, swap(near_other))
    weights += (swap(other_half([far_gate], LONG)), swap(other_half([far_up], LESS)))

    weights = [in_hbm(v) for v in weights]
    cot, _ = lax.optimization_barrier((cotangent, near_other))
    cot = cot.reshape(E, Z, X, 2, C * MOST, 128).transpose(3, 1, 2, 0, 4, 5)
    cot = cot.reshape(2, slots, 128)
    near_cot, far_cot = pick(cot, xl, 0), along_x(pick(cot, 1 - xl, 0))

    rows_spec = pl.BlockSpec((M, BLOCK, piece), lambda i: (i, 0, 0))
    gathered = call(
        gather_kernel,
        (1,),
        [whole(E * C, MOST + 1, piece)],
        whole(Y * M, BLOCK, piece),
        HBM((Y * M, BLOCK, piece), bf16),
        [pltpu.VMEM((BLOCK, piece), bf16)],
    )(arrived)
    rows = a2a(gathered, ("sect", "zl", "xh"))

    rows, near_cot, far_cot = lax.optimization_barrier((rows, near_cot, far_cot))

    def w_specs(rows, count):
        own = pl.BlockSpec((rows, 128), lambda i, place: (place[0] * count + i, 0))
        core = [pl.BlockSpec((n, rows, 128), lambda i, place: (0, i, 0)) for n in (2, 1, 1)]
        return [own] * 4 + core

    step_spec = pl.BlockSpec((M, BLOCK, piece), lambda i, place: (i, 0, 0))
    part = sds((slots, 512), f32)
    own, to_core = placed(
        pre_kernel,
        (1,),
        [whole(Y * M, BLOCK, piece)] + w_specs(half, 1),
        [whole(slots, 512), whole(slots, 512)],
        [part, part],
        [pltpu.VMEM((slots, half), bf16)],
    )(place, rows, *weights)
    hidden, far_hidden, d, coef = call(
        act_kernel,
        (1,),
        [smem]
        + [whole(slots, 512)] * 2
        + [whole(slots, 128)] * 2
        + [whole(M, BLOCK, piece)],
        [whole(slots, 128), whole(slots, 128), whole(slots, 640), whole(slots, 128)],
        [sds((slots, 128), bf16)] * 2 + [sds((slots, 640), bf16), sds((slots, 128), f32)],
    )(expert.reshape(1).astype(i32), own, swap(to_core), near_cot, far_cot, rows)

    back = placed(
        dx_kernel,
        (Y,),
        [whole(slots, 640)] * 2 + [whole(slots, 128)] + w_specs(piece, Y) + [step_spec],
        step_spec,
        HBM((Y * M, BLOCK, piece), bf16),
        [pltpu.VMEM((32, slots), bf16), pltpu.VMEM((2 * M, 128), f32)],
    )(place, d, swap(d), coef, *weights, rows)

    hidden_back = along_x(far_hidden)
    back = a2a(back, ("sect", "zl", "xh"))
    summed = call(
        sum_kernel,
        (Y,),
        [rows_spec],
        whole(E * C * 8, 512),
        sds((E * C * 8, 512), bf16),
        [pltpu.VMEM((BLOCK, piece), f32)],
    )(back)
    pairs = routes.reshape(-1)
    count = tok * 2
    same = pairs[:, None] == pairs[None, :]
    earlier = jnp.arange(count)[None, :] < jnp.arange(count)[:, None]
    ranks = jnp.sum((same & earlier).astype(i32), axis=1)
    places = pairs * MOST + ranks
    select = (places[None, :] == jnp.arange(E * MOST, dtype=i32)[:, None]).astype(f32)
    spread = jnp.sum(select.reshape(E * MOST, tok, 2), axis=2).astype(bf16)
    spread = spread.T.reshape(tok, E, MOST)
    choose = (routes[:, :, None] == jnp.arange(E, dtype=i32)[None, None, :]).astype(f32)
    probs = jax.nn.softmax(jnp.sum(choose * logits[:, None, :], axis=2), axis=1)
    w_mine = pick(w_router.reshape(C, Y, piece, E), sect, 1).astype(f32)

    summed, hidden_back, select, spread, choose, probs, w_mine = lax.optimization_barrier(
        (summed, hidden_back, select, spread, choose, probs, w_mine)
    )
    home = a2a(summed.reshape(E * C, 8, 512), ("e", "core"))
    home = home.reshape(E, C, 8, 512)

    mine = xl == jnp.arange(2)[:, None, None]
    hidden = jnp.where(mine, hidden[None], hidden_back[None])
    hidden = hidden.reshape(2, Z, X, E, C * MOST, 128).transpose(3, 1, 2, 0, 4, 5)
    hidden = hidden.reshape(2 * slots, 128)

    router = call(
        router_kernel,
        (1,),
        [whole(E * C, 8, 512)],
        whole(2 * M * C, C, piece),
        sds((2 * M * C, C, piece), f32),
    )(home.reshape(E * C, 8, 512))
    router = a2a(router, ("xl", "zl", "xh", "core"))

    tails = [home[:, :, 3, 0:256], home[:, :, 3, 256:512], home[:, :, 4, 0:256]]
    main = jnp.concatenate([home[:, :, 0:3, :], jnp.stack(tails, axis=2)], axis=3)
    token_dx = jnp.einsum("ter,ecrd->tcd", spread, main, preferred_element_type=f32)
    dp = jnp.sum(home[:, :, 7, 256:512].astype(f32), axis=1)
    dp = dp[:, 0:128] + dp[:, 128:256]
    dp = lax.dynamic_slice_in_dim(dp, (expert * C + core) * MOST, MOST, 1).reshape(E * MOST)
    pair_dp = jnp.sum(select * dp[:, None], axis=0).reshape(tok, 2)
    mean_dp = jnp.sum(probs * pair_dp, axis=1, keepdims=True)
    d_pick = probs * (pair_dp - mean_dp)
    d_logits = jnp.sum(choose * d_pick[:, :, None], axis=1)
    router_dx = jnp.einsum("te,cde->tcd", d_logits, w_mine, precision=lax.Precision.HIGHEST)
    grad_tokens = (token_dx + router_dx).astype(bf16).reshape(tok, C * piece)

    packed = call(
        pack_kernel,
        (1,),
        [whole(tok, C * piece), whole(2 * E, C, piece)],
        whole(Y, tok + 2 * E, C * piece),
        sds((Y, tok + 2 * E, C * piece), bf16),
    )(grad_tokens, router)
    grad_tokens, grad_router = call(
        last_kernel,
        (1,),
        [whole(Y, tok + 2 * E, C * piece)],
        [whole(tok, width), whole(E, width)],
        [sds((tok, width), bf16), sds((E, width), f32)],
    )(a2a(packed, ("sect",)))
    return hidden, grad_tokens, grad_router.T


def solution(mesh):
    fine = Mesh(mesh.devices.reshape(Y, E, Z, X, 2, C), AXES)
    seq = ("e", "zl", "xh", "xl", "core")
    columns = P(None, seq + ("sect",))
    return jax.shard_map(
        local,
        mesh=fine,
        in_specs=(P(seq, None), P(seq, None), P(), columns, columns, columns),
        out_specs=(columns, P(seq, None), P()),
        check_vma=False,
    )
```

```python
import jax
import jax.numpy as jnp
from jax import lax
from jax.experimental import pallas as pl
from jax.experimental.pallas import tpu as pltpu
from jax.sharding import Mesh, PartitionSpec as P

AXES = ("sect", "e", "zl", "xh", "xl", "core")
HBM = pltpu.MemorySpace.HBM
bf16, f32, i32 = jnp.bfloat16, jnp.float32, jnp.int32
Y, E, Z, X, C = 4, 8, 2, 2, 2
M = Z * X
MOST = 3
GROUP = E * C * MOST
BLOCK = GROUP + 8
LIMIT = 48 * 1024 * 1024
MOST_VMEM = 60 * 1024 * 1024
LONG = pl.CostEstimate(flops=40_000_000_000, bytes_accessed=100_000_000, transcendentals=0)
LESS = pl.CostEstimate(flops=22_000_000_000, bytes_accessed=10_000_000, transcendentals=0)


def iota(shape, dim):
    return lax.broadcasted_iota(i32, shape, dim)


def split2(v):
    hi = v.astype(bf16).astype(f32)
    return hi, v - hi


def route_kernel(place_ref, routes_ref, tokens_ref, router_ref, out_ref, logits_ref):
    tok = tokens_ref.shape[0]
    piece = out_ref.shape[-1]
    sect = place_ref[0]
    logits = lax.dot_general(
        tokens_ref[...], router_ref[...], (((1,), (1,)), ((), ())), preferred_element_type=f32
    )
    logits_ref[...] = logits
    row, lane = iota((tok, E), 0), iota((tok, E), 1)
    chosen = []
    for k in range(2):
        named = jnp.zeros((tok, E), i32)
        for t in range(tok):
            named = jnp.where(row == t, routes_ref[k, t], named)
        chosen.append(jnp.sum(jnp.where(lane == named, logits, 0.0), axis=1, keepdims=True))
    top = jnp.maximum(chosen[0], chosen[1])
    a, b = jnp.exp(chosen[0] - top), jnp.exp(chosen[1] - top)
    probs = [a / (a + b), b / (a + b)]
    hi, lo = split2(probs[0] * probs[1])

    pairs = [(t, k, routes_ref[k, t], routes_ref[1 - k, t]) for t in range(tok) for k in range(2)]
    ranks = []
    for i, pair in enumerate(pairs):
        rank = jnp.int32(0)
        for j in range(i):
            rank = rank + (pairs[j][2] == pair[2]).astype(i32)
        ranks.append(rank)

    rows8, lanes8 = iota((E, 128), 0), iota((E, 128), 1)
    meta = jnp.zeros((E, 128), f32)
    for (t, k, expert, other), rank in zip(pairs, ranks):
        here = rows8 == expert
        meta = jnp.where(here & (lanes8 == rank), (other + 1).astype(f32), meta)
        for q, value in ((1, probs[k]), (2, hi), (3, lo)):
            meta = jnp.where(here & (lanes8 == q * MOST + rank), value[t : t + 1, :], meta)
    meta = jnp.concatenate([meta, jnp.zeros((E, piece - 128), f32)], axis=1)

    rows_e = iota((E, piece), 0)
    for c in range(C):
        start = pl.multiple_of((c * Y + sect) * piece, 128)
        mine = tokens_ref[:, pl.ds(start, piece)].astype(f32)
        acc = [jnp.zeros((E, piece), f32) for _ in range(MOST)]
        for (t, _, expert, _), rank in zip(pairs, ranks):
            value = jnp.broadcast_to(mine[t : t + 1, :], (E, piece))
            for r in range(MOST):
                there = rows_e == jnp.where(rank == r, expert, -1)
                acc[r] = jnp.where(there, value, acc[r])
        for e in range(E):
            rows = [v[e : e + 1] for v in (*acc, meta)]
            out_ref[e, c] = jnp.concatenate(rows, axis=0).astype(bf16)


def gather_kernel(arrived_ref, out_ref, block_ref):
    @pl.when(pl.program_id(0) == 0)
    def _():
        count = E * C
        flat = jnp.concatenate([arrived_ref[j].astype(f32) for j in range(count)], axis=0)
        flat = flat.astype(bf16)
        slot, source = iota((GROUP, 4 * count), 0), iota((GROUP, 4 * count), 1)
        pick = jnp.where(source == slot // MOST * 4 + slot % MOST, 1.0, 0.0).astype(bf16)
        block_ref[0:GROUP, :] = jnp.dot(pick, flat, preferred_element_type=f32).astype(bf16)
        pick = jnp.where(source == slot // MOST * 4 + MOST, 1.0, 0.0).astype(bf16)
        notes = jnp.dot(pick, flat[:, 0:128], preferred_element_type=f32)
        slot, lane = iota((GROUP, 128), 0), iota((GROUP, 128), 1)
        rows = []
        for q in range(4):
            column = jnp.sum(
                jnp.where(lane == q * MOST + slot % MOST, notes, 0.0), axis=1, keepdims=True
            )
            rows.append(jnp.sum(jnp.where(lane == slot, column, 0.0), axis=0, keepdims=True))
        rows.append(jnp.zeros((4, 128), f32))
        rest = jnp.zeros((8, block_ref.shape[1] - 128), f32)
        notes = jnp.concatenate([jnp.concatenate(rows, axis=0), rest], axis=1)
        block_ref[GROUP:BLOCK, :] = notes.astype(bf16)

    for i in range(Y * M):
        out_ref[i] = block_ref[...]


def gathered_rows(rows_ref):
    return jnp.concatenate([rows_ref[i, 0:GROUP, :] for i in range(M)], axis=0)


def side(refs):
    own, near, gate, up = refs[0:4], refs[4], refs[5], refs[6]
    parts = [v[...] for v in own] + [near[0], near[1], gate[0], up[0]]
    return [jnp.concatenate(parts[i : i + 2], axis=1) for i in range(0, 8, 2)]


def half_kernel(place_ref, *refs):
    for i, ref in enumerate(refs[:-1]):
        refs[-1][i] = ref[...]


def pre_kernel(place_ref, rows_ref, *refs):
    weights, (own_ref, core_ref, flat_ref) = side(refs[0:7]), refs[7:10]
    width = rows_ref.shape[2]
    for y in range(Y):
        for i in range(M):
            flat_ref[i * GROUP : (i + 1) * GROUP, y * width : (y + 1) * width] = rows_ref[
                y * M + i, 0:GROUP, :
            ]
    for out, start, part in zip(
        (own_ref, own_ref, core_ref, core_ref), (0, 256, 0, 256), weights
    ):
        out[:, start : start + 256] = jnp.dot(flat_ref[...], part, preferred_element_type=f32)


def act_kernel(
    expert_ref, own_ref, core_ref, cot_ref, far_cot_ref, rows_ref, hidden_ref, far_ref, d_ref, coef_ref
):
    slots = own_ref.shape[0]
    eye = iota((GROUP, 128), 0) == iota((GROUP, 128), 1)

    def column(q):
        parts = []
        for i in range(M):
            notes = rows_ref[i, GROUP:BLOCK, 0:128].astype(f32)
            parts.append(jnp.sum(jnp.where(eye, notes[q : q + 1], 0.0), axis=1, keepdims=True))
        return jnp.concatenate(parts, axis=0)

    other = (column(0) - 1.0).astype(i32)
    weight = column(1)
    both = column(2) + column(3)
    dp = jnp.zeros((slots, 1), f32)
    for i, (cot, out) in enumerate(((cot_ref, hidden_ref), (far_cot_ref, far_ref))):
        first = slice(i * 256, i * 256 + 128)
        second = slice(i * 256 + 128, i * 256 + 256)
        gate = own_ref[:, first] + core_ref[:, first]
        up = own_ref[:, second] + core_ref[:, second]
        sigma = jax.nn.sigmoid(gate)
        act = gate * sigma * up
        out[...] = (weight * act).astype(bf16)
        grad_out = cot[...].astype(f32)
        dp = dp + jnp.sum(grad_out * act, axis=1, keepdims=True)
        d_gate = grad_out * weight * up * sigma * (1.0 + gate * (1.0 - sigma))
        d_up = grad_out * weight * gate * sigma
        d_ref[:, first] = d_gate.astype(bf16)
        d_ref[:, second] = d_up.astype(bf16)
    hi, rest = split2(dp)
    lo, last = split2(rest)
    lane = iota((slots, 128), 1)
    d_ref[:, 512:640] = jnp.where(
        lane == 0, hi, jnp.where(lane == 1, lo, jnp.where(lane == 2, last, 0.0))
    ).astype(bf16)
    third = lane % E
    sign = jnp.where(third == expert_ref[0], 1.0, 0.0) - jnp.where(third == other, 1.0, 0.0)
    coef_ref[...] = jnp.where(lane < 3 * E, sign * both, 0.0)


def dx_kernel(place_ref, own_ref, core_ref, coef_ref, *refs):
    weights, (rows_ref, out_ref, three_ref, dp_ref) = side(refs[0:7]), refs[7:11]
    slots = own_ref.shape[0]
    rows = gathered_rows(rows_ref)
    width = rows.shape[1]

    @pl.when(pl.program_id(0) == 0)
    def _():
        def dp_of(ref):
            return jnp.sum(ref[:, 512:640].astype(f32), axis=1, keepdims=True)

        dp = dp_of(own_ref)
        coef = coef_ref[...] * (dp + dp_of(core_ref))
        hi, rest = split2(coef)
        lo, last = split2(rest)
        lane = iota((slots, 128), 1)
        three = jnp.where(lane < E, hi, jnp.where(lane < 2 * E, lo, last))
        three_ref[...] = three.T[0:32].astype(bf16)
        eye = iota((GROUP, 128), 0) == iota((GROUP, 128), 1)
        parts = []
        for i in range(M):
            for v in split2(dp[i * GROUP : (i + 1) * GROUP]):
                parts.append(jnp.sum(jnp.where(eye, v, 0.0), axis=0, keepdims=True))
        dp_ref[...] = jnp.concatenate(parts, axis=0)

    dims = (((1,), (1,)), ((), ()))
    dx = None
    for d_ref, start, part in zip(
        (own_ref, own_ref, core_ref, core_ref), (0, 256, 0, 256), weights
    ):
        d = d_ref[:, start : start + 256]
        got = lax.dot_general(d, part, dims, preferred_element_type=f32)
        dx = got if dx is None else dx + got
    got = jnp.dot(three_ref[...], rows, preferred_element_type=f32)
    router = got[0:E] + got[E : 2 * E] + got[2 * E : 3 * E]
    router_hi, router_lo = split2(router)
    for i in range(M):
        out_ref[i, 0:GROUP, :] = dx[i * GROUP : (i + 1) * GROUP].astype(bf16)
        dp_rows = jnp.concatenate(
            [dp_ref[2 * i : 2 * i + 2], jnp.zeros((2, width - 128), f32)], axis=1
        )
        meta = [router_hi[2 * i : 2 * i + 2], router_lo[2 * i : 2 * i + 2], dp_rows]
        meta = jnp.concatenate([*meta, jnp.zeros((2, width), f32)], axis=0)
        out_ref[i, GROUP:BLOCK, :] = meta.astype(bf16)


def sum_kernel(recv_ref, out_ref, acc_ref):
    step = pl.program_id(0)
    total = jnp.sum(recv_ref[...].astype(f32), axis=0)

    @pl.when(step == 0)
    def _():
        acc_ref[...] = total

    @pl.when(step != 0)
    def _():
        acc_ref[...] += total

    @pl.when(step == pl.num_programs(0) - 1)
    def _():
        meta = acc_ref[GROUP:BLOCK, :]
        router_hi, router_lo = split2(meta[0:2] + meta[2:4])
        dp_hi, dp_lo = split2(meta[4:5, 0:128] + meta[5:6, 0:128])
        dp_row = jnp.concatenate([jnp.zeros((1, 512), f32), dp_hi, dp_lo], axis=1)
        source = jnp.concatenate(
            [acc_ref[0:GROUP, :], router_hi, router_lo, dp_row, jnp.zeros((3, 768), f32)], axis=0
        ).astype(bf16)
        shape = (E * C * 8, BLOCK)
        column = iota(shape, 1)
        place, q = iota(shape, 0) // 8, iota(shape, 0) % 8
        hi, lo, dp = GROUP + place % 2, GROUP + 2 + place % 2, jnp.full(shape, GROUP + 4, i32)

        def pick_rows(cases):
            target = jnp.full(shape, -1, i32)
            for value, where in cases:
                target = jnp.where(q == value, where, target)
            return jnp.where(column == target, 1.0, 0.0).astype(bf16)

        slot = MOST * place
        first = pick_rows([(0, slot), (1, slot + 1), (2, slot + 2), (5, hi), (6, lo)])
        left = pick_rows([(3, slot), (4, slot + 2), (7, lo)])
        right = pick_rows([(3, slot + 1), (4, hi), (7, dp)])
        got = jnp.dot(first, source[:, 0:512], preferred_element_type=f32)
        tail = source[:, 512:768]
        out_ref[:, 0:256] = (
            got[:, 0:256] + jnp.dot(left, tail, preferred_element_type=f32)
        ).astype(bf16)
        out_ref[:, 256:512] = (
            got[:, 256:512] + jnp.dot(right, tail, preferred_element_type=f32)
        ).astype(bf16)


def router_kernel(home_ref, out_ref):
    rows = []
    for c in range(C):
        total = home_ref[c].astype(f32)
        for e in range(1, E):
            total = total + home_ref[e * C + c].astype(f32)
        rest = total[4:5, 256:512] + total[7:8, 0:256]
        rows.append(jnp.concatenate([total[5:6] + total[6:7], rest], axis=1))
    rows = jnp.concatenate(rows, axis=0)
    for i in range(out_ref.shape[0]):
        out_ref[i] = rows


def pack_kernel(tokens_ref, router_ref, out_ref):
    piece = router_ref.shape[2]
    for c in range(C):
        part = slice(c * piece, (c + 1) * piece)
        total = router_ref[0:E, c, :] + router_ref[E : 2 * E, c, :]
        hi, lo = split2(total)
        block = jnp.concatenate([tokens_ref[:, part].astype(f32), hi, lo], axis=0).astype(bf16)
        for y in range(Y):
            out_ref[y, :, part] = block


def last_kernel(got_ref, tokens_ref, router_ref):
    tok = tokens_ref.shape[0]
    piece = got_ref.shape[2] // C
    for y in range(Y):
        for c in range(C):
            block = got_ref[y, :, c * piece : (c + 1) * piece].astype(f32)
            part = slice((c * Y + y) * piece, (c * Y + y + 1) * piece)
            tokens_ref[:, part] = block[0:tok].astype(bf16)
            router_ref[:, part] = block[tok : tok + E] + block[tok + E :]


def call(kernel, grid, in_specs, out_specs, out_shape, scratch=(), limit=LIMIT):
    return pl.pallas_call(
        kernel,
        grid=grid,
        in_specs=in_specs,
        out_specs=out_specs,
        out_shape=out_shape,
        scratch_shapes=list(scratch),
        compiler_params=pltpu.CompilerParams(vmem_limit_bytes=limit),
    )


def placed(kernel, grid, in_specs, out_specs, out_shape, scratch=(), cost=None):
    return pl.pallas_call(
        kernel,
        grid_spec=pltpu.PrefetchScalarGridSpec(
            num_scalar_prefetch=1,
            grid=grid,
            in_specs=in_specs,
            out_specs=out_specs,
            scratch_shapes=list(scratch),
        ),
        out_shape=out_shape,
        compiler_params=pltpu.CompilerParams(vmem_limit_bytes=LIMIT),
        cost_estimate=cost,
    )


def whole(*shape):
    return pl.BlockSpec(shape, lambda *_: (0,) * len(shape))


def in_hbm(v):
    return pltpu.with_memory_space_constraint(v, HBM)


def a2a(v, axes):
    return lax.all_to_all(v, axes, split_axis=0, concat_axis=0, tiled=True)


def everywhere(v, count):
    return jnp.broadcast_to(v[None], (count,) + v.shape)


def swap(v):
    return lax.ppermute(v, "core", [(0, 1), (1, 0)])


def along_x(v):
    order = []
    for x in range(2 * X):
        for c in range(C):
            order.append((x * C + c, (x ^ 1 if c == 0 else 2 * X - 1 - x) * C + c))
    return lax.ppermute(v, ("xh", "xl", "core"), order)


def pick(v, index, axis):
    return lax.dynamic_index_in_dim(v, index, axis=axis, keepdims=False)


def local(tokens, routes, w_router, w_gate, w_up, cotangent):
    tok, width = tokens.shape
    half, piece = width // C, width // (C * Y)
    core, xl, sect = lax.axis_index("core"), lax.axis_index("xl"), lax.axis_index("sect")
    expert = lax.axis_index("e")
    slots = cotangent.shape[0] // 2
    sds = jax.ShapeDtypeStruct
    smem = pl.BlockSpec(memory_space=pltpu.SMEM)

    far_gate, far_up = along_x(w_gate), along_x(w_up)

    message, logits = call(
        route_kernel,
        (1,),
        [smem, smem, whole(tok, width), whole(E, width)],
        [whole(E, C, MOST + 1, piece), whole(tok, E)],
        [sds((E, C, MOST + 1, piece), bf16), sds((tok, E), f32)],
        limit=MOST_VMEM,
    )(sect.reshape(1).astype(i32), routes.T, tokens, w_router.T)
    arrived = a2a(message.reshape(E * C, MOST + 1, piece), ("e", "core"))

    place = core.reshape(1).astype(i32)

    def other_half(parts, cost=None):
        block = pl.BlockSpec((half, 128), lambda i, place: (1 - place[0], 0))
        return pl.pallas_call(
            half_kernel,
            grid_spec=pltpu.PrefetchScalarGridSpec(
                num_scalar_prefetch=1,
                grid=(1,),
                in_specs=[block] * len(parts),
                out_specs=whole(len(parts), half, 128),
            ),
            out_shape=sds((len(parts), half, 128), bf16),
            compiler_params=pltpu.CompilerParams(vmem_limit_bytes=LIMIT),
            cost_estimate=cost,
        )(place, *parts)

    near_other = other_half([in_hbm(w_gate), in_hbm(w_up)])
    weights = (w_gate, w_up, far_gate, far_up, swap(near_other))
    weights += (swap(other_half([far_gate], LONG)), swap(other_half([far_up], LESS)))

    weights = [in_hbm(v) for v in weights]
    cot, _ = lax.optimization_barrier((cotangent, near_other))
    cot = cot.reshape(E, Z, X, 2, C * MOST, 128).transpose(3, 1, 2, 0, 4, 5)
    cot = cot.reshape(2, slots, 128)
    near_cot, far_cot = pick(cot, xl, 0), along_x(pick(cot, 1 - xl, 0))

    rows_spec = pl.BlockSpec((M, BLOCK, piece), lambda i: (i, 0, 0))
    gathered = call(
        gather_kernel,
        (1,),
        [whole(E * C, MOST + 1, piece)],
        whole(Y * M, BLOCK, piece),
        HBM((Y * M, BLOCK, piece), bf16),
        [pltpu.VMEM((BLOCK, piece), bf16)],
    )(arrived)
    rows = a2a(gathered, ("sect", "zl", "xh"))

    rows, near_cot, far_cot = lax.optimization_barrier((rows, near_cot, far_cot))

    def w_specs(rows, count):
        own = pl.BlockSpec((rows, 128), lambda i, place: (place[0] * count + i, 0))
        core = [pl.BlockSpec((n, rows, 128), lambda i, place: (0, i, 0)) for n in (2, 1, 1)]
        return [own] * 4 + core

    step_spec = pl.BlockSpec((M, BLOCK, piece), lambda i, place: (i, 0, 0))
    part = sds((slots, 512), f32)
    own, to_core = placed(
        pre_kernel,
        (1,),
        [whole(Y * M, BLOCK, piece)] + w_specs(half, 1),
        [whole(slots, 512), whole(slots, 512)],
        [part, part],
        [pltpu.VMEM((slots, half), bf16)],
    )(place, rows, *weights)
    hidden, far_hidden, d, coef = call(
        act_kernel,
        (1,),
        [smem]
        + [whole(slots, 512)] * 2
        + [whole(slots, 128)] * 2
        + [whole(M, BLOCK, piece)],
        [whole(slots, 128), whole(slots, 128), whole(slots, 640), whole(slots, 128)],
        [sds((slots, 128), bf16)] * 2 + [sds((slots, 640), bf16), sds((slots, 128), f32)],
    )(expert.reshape(1).astype(i32), own, swap(to_core), near_cot, far_cot, rows)

    back = placed(
        dx_kernel,
        (Y,),
        [whole(slots, 640)] * 2 + [whole(slots, 128)] + w_specs(piece, Y) + [step_spec],
        step_spec,
        HBM((Y * M, BLOCK, piece), bf16),
        [pltpu.VMEM((32, slots), bf16), pltpu.VMEM((2 * M, 128), f32)],
    )(place, d, swap(d), coef, *weights, rows)

    hidden_back = along_x(far_hidden)
    back = a2a(back, ("sect", "zl", "xh"))
    summed = call(
        sum_kernel,
        (Y,),
        [rows_spec],
        whole(E * C * 8, 512),
        sds((E * C * 8, 512), bf16),
        [pltpu.VMEM((BLOCK, piece), f32)],
    )(back)
    pairs = routes.reshape(-1)
    count = tok * 2
    same = pairs[:, None] == pairs[None, :]
    earlier = jnp.arange(count)[None, :] < jnp.arange(count)[:, None]
    ranks = jnp.sum((same & earlier).astype(i32), axis=1)
    places = pairs * MOST + ranks
    select = (places[None, :] == jnp.arange(E * MOST, dtype=i32)[:, None]).astype(f32)
    spread = jnp.sum(select.reshape(E * MOST, tok, 2), axis=2).astype(bf16)
    spread = spread.T.reshape(tok, E, MOST)
    choose = (routes[:, :, None] == jnp.arange(E, dtype=i32)[None, None, :]).astype(f32)
    probs = jax.nn.softmax(jnp.sum(choose * logits[:, None, :], axis=2), axis=1)
    w_mine = pick(w_router.reshape(C, Y, piece, E), sect, 1).astype(f32)

    summed, hidden_back, select, spread, choose, probs, w_mine = lax.optimization_barrier(
        (summed, hidden_back, select, spread, choose, probs, w_mine)
    )
    home = a2a(summed.reshape(E * C, 8, 512), ("e", "core"))
    home = home.reshape(E, C, 8, 512)

    mine = xl == jnp.arange(2)[:, None, None]
    hidden = jnp.where(mine, hidden[None], hidden_back[None])
    hidden = hidden.reshape(2, Z, X, E, C * MOST, 128).transpose(3, 1, 2, 0, 4, 5)
    hidden = hidden.reshape(2 * slots, 128)

    router = call(
        router_kernel,
        (1,),
        [whole(E * C, 8, 512)],
        whole(2 * M * C, C, piece),
        sds((2 * M * C, C, piece), f32),
    )(home.reshape(E * C, 8, 512))
    router = a2a(router, ("xl", "zl", "xh", "core"))

    tails = [home[:, :, 3, 0:256], home[:, :, 3, 256:512], home[:, :, 4, 0:256]]
    main = jnp.concatenate([home[:, :, 0:3, :], jnp.stack(tails, axis=2)], axis=3)
    token_dx = jnp.einsum("ter,ecrd->tcd", spread, main, preferred_element_type=f32)
    dp = jnp.sum(home[:, :, 7, 256:512].astype(f32), axis=1)
    dp = dp[:, 0:128] + dp[:, 128:256]
    dp = lax.dynamic_slice_in_dim(dp, (expert * C + core) * MOST, MOST, 1).reshape(E * MOST)
    pair_dp = jnp.sum(select * dp[:, None], axis=0).reshape(tok, 2)
    mean_dp = jnp.sum(probs * pair_dp, axis=1, keepdims=True)
    d_pick = probs * (pair_dp - mean_dp)
    d_logits = jnp.sum(choose * d_pick[:, :, None], axis=1)
    router_dx = jnp.einsum("te,cde->tcd", d_logits, w_mine, precision=lax.Precision.HIGHEST)
    grad_tokens = (token_dx + router_dx).astype(bf16).reshape(tok, C * piece)

    packed = call(
        pack_kernel,
        (1,),
        [whole(tok, C * piece), whole(2 * E, C, piece)],
        whole(Y, tok + 2 * E, C * piece),
        sds((Y, tok + 2 * E, C * piece), bf16),
    )(grad_tokens, router)
    grad_tokens, grad_router = call(
        last_kernel,
        (1,),
        [whole(Y, tok + 2 * E, C * piece)],
        [whole(tok, width), whole(E, width)],
        [sds((tok, width), bf16), sds((E, width), f32)],
    )(a2a(packed, ("sect",)))
    return hidden, grad_tokens, grad_router.T


def solution(mesh):
    fine = Mesh(mesh.devices.reshape(Y, E, Z, X, 2, C), AXES)
    seq = ("e", "zl", "xh", "xl", "core")
    columns = P(None, seq + ("sect",))
    return jax.shard_map(
        local,
        mesh=fine,
        in_specs=(P(seq, None), P(seq, None), P(), columns, columns, columns),
        out_specs=(columns, P(seq, None), P()),
        check_vma=False,
    )
```
